512 devices in a mesh: row: 32 (over x, y, core), col: 16 (over z).
Axes of the slice: x: 4, y: 4, z: 16, core: 2. Of those that a mesh axis runs over, the one named last changes fastest.
Arguments:
- inputs: bfloat16 [2048, 6144], P('row', 'col'), may hold values from -6 to 6
- out_grad: bfloat16 [2048, 6144], P('row', 'col'), may hold values from -6 to 6
- preact: bfloat16 [2048, 12288], P('col', 'row'), may hold values from -6 to 6
- weight_in: bfloat16 [6144, 12288], P('col', 'row'), may hold values from -0.078125 to 0.078125
- weight_out: bfloat16 [12288, 6144], P('row', 'col'), may hold values from -0.0546875 to 0.0546875
- moment_in: bfloat16 [6144, 12288], P('col', 'row'), may hold values from -3 to 3
- second_in: bfloat16 [6144, 12288], P('col', 'row'), may hold values from 0.049804688 to 5
- moment_out: bfloat16 [12288, 6144], P('row', 'col'), may hold values from -3 to 3
- second_out: bfloat16 [12288, 6144], P('row', 'col'), may hold values from 0.049804688 to 5
Outputs:
- input_grad: bfloat16 [2048, 6144], P('row', 'col')
- new_weight_in: bfloat16 [6144, 12288], P('col', 'row')
- new_moment_in: bfloat16 [6144, 12288], P('col', 'row')
- new_second_in: bfloat16 [6144, 12288], P('col', 'row')
- new_weight_out: bfloat16 [12288, 6144], P('row', 'col')
- new_moment_out: bfloat16 [12288, 6144], P('row', 'col')
- new_second_out: bfloat16 [12288, 6144], P('row', 'col')
The draws below stay inside these ranges and needn't reach their ends.
All inputs are finite; a program needn't handle non-finite values.
Results may differ from the reference program's by a relative error of at most 0.03.
Values may be sent and summed in bfloat16 or wider, within the bound.
A program may use at most 64 MiB of HBM per device.

```python
import math
import jax
import jax.numpy as jnp
from jax import lax

D = 6144
FF = 12288
TOKENS = 2048
N_ROW = 32
N_COL = 16


def levels(own_key, extent, pieces, smallest, top_value):
    loudness = 1.0
    for axis_at, parts in pieces:
        steps = jax.random.uniform(jax.random.fold_in(jax.random.fold_in(own_key, 6), axis_at), (parts,), jnp.float32, smallest / len(pieces), top_value / len(pieces))
        loudness = loudness * jnp.repeat(jnp.exp(steps), extent[axis_at] // parts).reshape((-1,) + (1,) * (len(extent) - 1 - axis_at))
    return loudness


def gaussian(key, extent, scale, most, shards=(), held_as=jnp.bfloat16):
    factor_of = levels(key, extent, shards, -0.22, 0.18) if shards else 1.0
    result = jax.random.normal(key, extent, jnp.float32) * scale * factor_of
    return jnp.minimum(jnp.maximum(result, -most), most).astype(held_as)


def setup_inputs(seed: int = 0) -> dict:
    seeds = jax.random.split(jax.random.key(seed), 10)
    inputs = gaussian(seeds[0], (TOKENS, D), 1.0, 6.0, ((0, 32), (1, 16)))
    out_grad = gaussian(seeds[1], (TOKENS, D), 1.0, 6.0, ((0, 32), (1, 16)))
    preact = gaussian(seeds[2], (TOKENS, FF), 1.0, 6.0, ((0, 16), (1, 32)))
    weight_in = gaussian(seeds[3], (D, FF), D ** -0.5, 0.078125, ((0, 16), (1, 32)))
    weight_out = gaussian(seeds[4], (FF, D), FF ** -0.5, 0.0546875, ((0, 32), (1, 16)))
    moment_in = gaussian(seeds[5], (D, FF), 0.5, 3.0, ((0, 16), (1, 32)))
    second_in = jnp.clip(jnp.exp(math.log(5.0) - 4.609084 * jax.random.uniform(seeds[6], (D, FF), jnp.float32) ** levels(seeds[6], (D, FF), ((0, 16), (1, 32)), -0.2, 0.2)), 0.049804688, 5.0).astype(jnp.bfloat16)
    moment_out = gaussian(seeds[7], (FF, D), 0.5, 3.0, ((0, 32), (1, 16)))
    second_out = jnp.clip(jnp.exp(math.log(5.0) - 4.609084 * jax.random.uniform(seeds[8], (FF, D), jnp.float32) ** levels(seeds[8], (FF, D), ((0, 32), (1, 16)), -0.2, 0.2)), 0.049804688, 5.0).astype(jnp.bfloat16)
    return {"inputs": inputs, "out_grad": out_grad, "preact": preact, "weight_in": weight_in, "weight_out": weight_out, "moment_in": moment_in, "second_in": second_in, "moment_out": moment_out, "second_out": second_out}


gelu_coef = 0.7978845608
beta_first = 0.9
beta_second = 0.95
learn_rate = 0.003
epsilon_adam = 1e-08
correct_first = 1.0 - 0.9 ** 10
correct_second = 1.0 - 0.95 ** 10

def gelu_parts(preact):
    values = preact.astype(jnp.float32)
    tangent = jnp.tanh(gelu_coef * (values + 0.044715 * values * values * values))
    activated = 0.5 * values * (1.0 + tangent)
    slopes = 0.5 * (1.0 + tangent) + 0.5 * values * (1.0 - tangent * tangent) * gelu_coef * (1.0 + 3.0 * 0.044715 * values * values)
    return (activated, slopes)

def adam_step(weight, moment, second, grads):
    first_new = beta_first * moment.astype(jnp.float32) + (1.0 - beta_first) * grads
    second_new = beta_second * second.astype(jnp.float32) + (1.0 - beta_second) * grads * grads
    weight_new = weight.astype(jnp.float32) - learn_rate * (first_new / correct_first) / (jnp.sqrt(second_new / correct_second) + epsilon_adam)
    return (weight_new.astype(jnp.bfloat16), first_new.astype(jnp.bfloat16), second_new.astype(jnp.bfloat16))

def rounded_sum(left, right, width, groups, rows, cols):

    def add_group(index, total):
        start = (index * width).astype(jnp.int32)
        left_part = lax.dynamic_slice_in_dim(left, start, width, 1)
        right_part = lax.dynamic_slice_in_dim(right, start, width, 1)
        partial_sum = lax.dot_general(left_part, right_part, (((1,), (1,)), ((), ())), preferred_element_type=jnp.float32)
        rounded = lax.optimization_barrier(partial_sum.astype(jnp.bfloat16))
        return total + rounded.astype(jnp.float32)
    return lax.fori_loop(0, groups, add_group, jnp.zeros((rows, cols), jnp.float32))

def reference(inputs, out_grad, preact, weight_in, weight_out, moment_in, second_in, moment_out, second_out):
    hidden_grad = rounded_sum(out_grad, weight_out, D // N_COL, N_COL, TOKENS, FF)
    activated, slopes = gelu_parts(preact)
    activated = activated.astype(jnp.bfloat16)
    hidden_delta = (hidden_grad * slopes).astype(jnp.bfloat16)
    grad_out = lax.dot_general(activated, out_grad, (((0,), (0,)), ((), ())), preferred_element_type=jnp.float32)
    grad_in = lax.dot_general(inputs, hidden_delta, (((0,), (0,)), ((), ())), preferred_element_type=jnp.float32)
    input_grad = rounded_sum(hidden_delta, weight_in, FF // N_ROW, N_ROW, TOKENS, D).astype(jnp.bfloat16)
    weight_a, moment_a, second_a = adam_step(weight_in, moment_in, second_in, grad_in)
    weight_b, moment_b, second_b = adam_step(weight_out, moment_out, second_out, grad_out)
    return (input_grad, weight_a, moment_a, second_a, weight_b, moment_b, second_b)
```

```python
import functools
import math

import jax
import jax.numpy as jnp
from jax import lax
from jax.experimental import pallas as pl
from jax.experimental.pallas import tpu as pltpu
from jax.sharding import PartitionSpec as P

gelu_coef = 0.7978845608
beta_first = 0.9
beta_second = 0.95
learn_rate = 0.003
epsilon_adam = 1e-08
correct_first = 1.0 - 0.9**10
correct_second = 1.0 - 0.95**10

MESH = pl.DeviceIdType.MESH
BF = jnp.bfloat16
F32 = jnp.float32
SUBS = 2


def gelu_parts(preact):
    values = preact.astype(jnp.float32)
    tangent = jnp.tanh(gelu_coef * (values + 0.044715 * values * values * values))
    activated = 0.5 * values * (1.0 + tangent)
    slopes = 0.5 * (1.0 + tangent) + 0.5 * values * (1.0 - tangent * tangent) * gelu_coef * (
        1.0 + 3.0 * 0.044715 * values * values
    )
    return (activated, slopes)


def adam_step(weight, moment, second, grads):
    first_new = beta_first * moment.astype(jnp.float32) + (1.0 - beta_first) * grads
    second_new = beta_second * second.astype(jnp.float32) + (1.0 - beta_second) * grads * grads
    weight_new = weight.astype(jnp.float32) - learn_rate * (first_new / correct_first) / (
        jnp.sqrt(second_new / correct_second) + epsilon_adam
    )
    return (
        weight_new.astype(jnp.bfloat16),
        first_new.astype(jnp.bfloat16),
        second_new.astype(jnp.bfloat16),
    )


def nt_dot(left, right):
    return lax.dot_general(left, right, (((1,), (1,)), ((), ())), preferred_element_type=F32)


def tn_dot(left, right):
    return lax.dot_general(left, right, (((0,), (0,)), ((), ())), preferred_element_type=F32)


class Plan:
    def __init__(self, n_row, n_col, tokens, features, hidden):
        self.nq = n_row // 2
        self.X = math.isqrt(self.nq)
        self.Y = self.nq // self.X
        self.nz = n_col
        self.long = n_col // 2
        self.short = n_col - 1 - self.long
        self.msgs = n_col - 1
        self.TL = tokens
        self.TB = 2 * tokens
        self.DL = features
        self.FL = hidden


def kernel(
    plan,
    og_ref,
    in_ref,
    pre_ref,
    win_ref,
    wout_ref,
    ig_ref,
    gin_ref,
    gout_ref,
    og_all,
    in_all,
    act_all,
    del_all,
    slopes,
    ring,
    sib_out,
    sib_in,
    own,
    rv_a,
    rv_b,
    st_a,
    st_b,
    fin_a,
    fin_b,
    act_s,
    act_r,
    rs_s,
    rs_r,
    del_s,
    del_r,
    og_own_s,
    og_a_s,
    og_b_s,
    og_a_r,
    og_b_r,
    og_sib_s,
    og_sib_r,
    in_own_s,
    in_a_s,
    in_b_s,
    in_a_r,
    in_b_r,
    in_sib_s,
    in_sib_r,
    sib_s,
    sib_r,
    ra_s,
    ra_r,
    rb_s,
    rb_r,
    fa_s,
    fa_r,
    fb_s,
    fb_r,
):
    X, Y, NZ, TL, TB = plan.X, plan.Y, plan.nz, plan.TL, plan.TB
    HALF, MSGS = TL // 2, plan.msgs
    SUB = TB // SUBS
    r = lax.axis_index("row")
    z = lax.axis_index("col")
    q = r // 2
    c = r % 2
    x = q // Y
    y = q % Y
    sgn = 1 - 2 * c
    sib = (r + sgn, z)

    def chip(cx, cy):
        return ((cx * Y + cy) * 2 + c, z)

    def x_peer(j):
        return (x + j) % X

    def y_peer(j):
        return (y + j) % Y

    def remote(src, dst, ssem, rsem, dev):
        return pltpu.make_async_remote_copy(
            src_ref=src, dst_ref=dst, send_sem=ssem, recv_sem=rsem, device_id=dev, device_id_type=MESH
        )

    def rows(buf, start, size):
        return buf.at[pl.ds(pl.multiple_of(start, 16), size)]

    def sign(n):
        return (1 - 2 * (n % 2)) * sgn

    def toward(n):
        return (r, (z + sign(n) + NZ) % NZ)

    def sent_block(n):
        return (z - sign(n) * (n // 2) + 2 * NZ) % NZ

    def got_block(n):
        return (z - sign(n) * (n // 2 + 1) + 2 * NZ) % NZ

    def rs_target(n):
        reach = plan.long - (n % 2) * (plan.long - plan.short)
        return (z + sign(n) * (reach - n // 2) + 2 * NZ) % NZ

    def ring_copy(buf, block, n, sub, ssem, rsem):
        part = rows(buf, block * TB + sub * SUB, SUB)
        return remote(part, part, ssem.at[n, sub], rsem.at[n, sub], toward(n))

    def ring_send(buf, n, ssem, rsem):
        for sub in range(SUBS):
            ring_copy(buf, sent_block(n), n, sub, ssem, rsem).start()

    def ring_pass(buf, n, ssem, rsem):
        for sub in range(SUBS):
            ring_copy(buf, got_block(n), n, sub, ssem, rsem).wait_recv()

            @pl.when(n + 2 < MSGS)
            def _():
                ring_copy(buf, sent_block(n + 2), n + 2, sub, ssem, rsem).start()

    def act_pass(n):
        ring_pass(act_all, n, act_s, act_r)

    def block_rows(buf, cx, cy, part=None, core=None):
        start = ((cx * Y + cy) * 2 + (c if core is None else core)) * TL
        if part is None:
            return rows(buf, start, TL)
        return rows(buf, start + part * HALF, HALF)

    def gather_ops(buf, own_s, a_s, b_s, a_r, b_r, s_s, s_r):
        def whole(j, along_x):
            part = block_rows(buf, x, y)
            if along_x:
                return remote(part, part, own_s.at[0, j - 1], a_r.at[q], chip(x_peer(j), y))
            return remote(part, part, own_s.at[1, j - 1], a_r.at[q], chip(x, y_peer(j)))

        def whole_got(cx, cy):
            part = block_rows(buf, cx, cy)
            return remote(part, part, own_s.at[0, 0], a_r.at[cx * Y + cy], sib)

        def pass_a(j, k):
            cx = x_peer(j)
            part = block_rows(buf, cx, y, 0)
            return remote(part, part, a_s.at[j - 1, k - 1], a_r.at[cx * Y + y], chip(x, y_peer(k)))

        def pass_b(j, k):
            cy = y_peer(j)
            part = block_rows(buf, x, cy, 1)
            return remote(part, part, b_s.at[j - 1, k - 1], b_r.at[x * Y + cy], chip(x_peer(k), y))

        def half_got(cx, cy, part, sem):
            half = block_rows(buf, cx, cy, part)
            return remote(half, half, own_s.at[0, 0], sem.at[cx * Y + cy], sib)

        def to_sib(cx, cy):
            part = block_rows(buf, cx, cy)
            at = cx * Y + cy
            return remote(part, part, s_s.at[at], s_r.at[at], sib)

        def from_sib(cx, cy):
            part = block_rows(buf, cx, cy, core=1 - c)
            at = cx * Y + cy
            return remote(part, part, s_s.at[at], s_r.at[at], sib)

        def first():
            for j in (1, X - 1) + tuple(range(2, X - 1)) if X > 2 else (1,):
                whole(j, True).start()
            for j in (1, Y - 1) + tuple(range(2, Y - 1)) if Y > 2 else (1,):
                whole(j, False).start()
            to_sib(x, y).start()

        def second():
            def step(j, _):
                whole_got(x_peer(j), y).wait_recv()
                for k in range(1, Y):
                    pass_a(j, k).start()
                whole_got(x, y_peer(j)).wait_recv()
                for k in range(1, X):
                    pass_b(j, k).start()
                to_sib(x_peer(j), y).start()
                to_sib(x, y_peer(j)).start()
                return 0

            lax.fori_loop(1, X, step, 0)

        def third():
            def step(i, _):
                cx = x_peer(i // (Y - 1) + 1)
                cy = y_peer(i % (Y - 1) + 1)
                half_got(cx, cy, 0, a_r).wait_recv()
                half_got(cx, cy, 1, b_r).wait_recv()
                to_sib(cx, cy).start()
                return 0

            lax.fori_loop(0, (X - 1) * (Y - 1), step, 0)

        def fourth():
            def step(i, _):
                from_sib(i // Y, i % Y).wait_recv()
                return 0

            lax.fori_loop(0, X * Y, step, 0)

        def sent():
            def step(j, _):
                whole(j, True).wait_send()
                whole(j, False).wait_send()
                for k in range(1, Y):
                    pass_a(j, k).wait_send()
                for k in range(1, X):
                    pass_b(j, k).wait_send()
                return 0

            lax.fori_loop(1, X, step, 0)

            def sib_step(i, _):
                to_sib(i // Y, i % Y).wait_send()
                return 0

            lax.fori_loop(0, X * Y, sib_step, 0)

        return first, second, third, fourth, sent

    og_ops = gather_ops(og_all, og_own_s, og_a_s, og_b_s, og_a_r, og_b_r, og_sib_s, og_sib_r)
    in_ops = gather_ops(in_all, in_own_s, in_a_s, in_b_s, in_a_r, in_b_r, in_sib_s, in_sib_r)

    barrier = pltpu.get_barrier_semaphore()
    friends = [sib, toward(0), toward(1)]
    friends += [chip(x_peer(j), y) for j in range(1, X)]
    friends += [chip(x, y_peer(j)) for j in range(1, Y)]
    for friend in friends:
        pl.semaphore_signal(barrier, inc=1, device_id=friend, device_id_type=MESH)
    mine = pl.ds(pl.multiple_of(r * TL, 16), TL)
    block = pl.ds(pl.multiple_of(z * TB, 16), TB)
    og_all[mine] = og_ref[...]
    in_all[mine] = in_ref[...]
    act, slope = gelu_parts(pre_ref[...])
    act_all[block] = act.astype(BF)
    slopes[...] = slope
    ring[0] = jnp.zeros((TB, plan.FL), BF)
    ring[1] = jnp.zeros((TB, plan.FL), BF)
    gin_ref[...] = jnp.zeros_like(gin_ref)
    gout_ref[...] = jnp.zeros_like(gout_ref)
    pl.semaphore_wait(barrier, len(friends))

    og_ops[0]()
    ring_send(act_all, 0, act_s, act_r)
    ring_send(act_all, 1, act_s, act_r)
    og_ops[1]()
    act_pass(0)
    act_pass(1)
    og_ops[2]()
    act_pass(2)
    act_pass(3)
    og_ops[3]()
    in_ops[0]()

    ACT0 = 4

    def rs_copy(n, sub):
        src = ring.at[n, pl.ds(sub * SUB, SUB)]
        dst = ring.at[n + 2, pl.ds(sub * SUB, SUB)]
        return remote(src, dst, rs_s.at[n, sub], rs_r.at[n, sub], toward(n))

    def rs_step(n, _):
        at = pl.multiple_of(rs_target(n) * TB, 16)
        part = nt_dot(og_all[pl.ds(at, TB)], wout_ref[...]).astype(BF).astype(F32)
        for sub in range(SUBS):
            here = pl.ds(sub * SUB, SUB)

            @pl.when(n >= 2)
            def _():
                rs_copy(n - 2, sub).wait_recv()

            ring[n, here] = (ring[n, here].astype(F32) + part[sub * SUB : (sub + 1) * SUB]).astype(BF)

            @pl.when(n < MSGS)
            def _():
                rs_copy(n, sub).start()

        @pl.when(n + ACT0 < MSGS)
        def _():
            act_pass(n + ACT0)

        @pl.when(n == 3)
        def _():
            in_ops[1]()

        @pl.when(n == 8)
        def _():
            in_ops[2]()

        return 0

    lax.fori_loop(0, NZ, rs_step, 0)
    for sub in range(SUBS):
        rs_copy(MSGS - 1, sub).wait_recv()
    total = ring[NZ - 1].astype(F32) + ring[NZ].astype(F32)
    del_all[block] = (total * slopes[...]).astype(BF)
    ring_send(del_all, 0, del_s, del_r)
    ring_send(del_all, 1, del_s, del_r)
    in_ops[3]()

    def chunk(i):
        sig = (2 * (i % 2) - 1) * sgn
        return (z - sig * ((i + 1) // 2) + 2 * NZ) % NZ

    def sib_copy(t):
        return remote(sib_out.at[t], sib_in.at[t], sib_s.at[t], sib_r.at[t], sib)

    low, high = pl.ds(0, HALF), pl.ds(HALF, HALF)

    def a_copy(t):
        tx, ty = t // Y, t % Y
        return remote(own.at[t, low], rv_a.at[ty, x], ra_s.at[t], ra_r.at[ty, x], chip(tx, y))

    def a_got(ty, sx):
        return remote(rv_a.at[ty, sx], rv_a.at[ty, sx], ra_s.at[0], ra_r.at[ty, sx], sib)

    def b_copy(t):
        tx, ty = t // Y, t % Y
        return remote(own.at[t, high], rv_b.at[tx, y], rb_s.at[t], rb_r.at[tx, y], chip(x, ty))

    def b_got(tx, sy):
        return remote(rv_b.at[tx, sy], rv_b.at[tx, sy], rb_s.at[0], rb_r.at[tx, sy], sib)

    def fa_copy(ty):
        return remote(st_a.at[ty], fin_a.at[y], fa_s.at[ty], fa_r.at[y], chip(x, ty))

    def fb_copy(tx):
        return remote(st_b.at[tx], fin_b.at[x], fb_s.at[tx], fb_r.at[x], chip(tx, y))

    def arrive(i):
        @pl.when(i >= 1)
        def _():
            ring_pass(del_all, i - 1, del_s, del_r)

        t = chunk(i)
        at = pl.multiple_of(t * TB, 16)
        theirs = pl.ds(pl.multiple_of(at + (1 - c) * TL, 16), TL)
        sib_out[t] = nt_dot(del_all[theirs], win_ref[...]).astype(BF)
        sib_copy(t).start()
        ours = pl.ds(pl.multiple_of(at + c * TL, 16), TL)
        own[t] = nt_dot(del_all[ours], win_ref[...]).astype(BF)
        here = pl.ds(at, TB)
        gin_ref[...] += tn_dot(in_all[here], del_all[here])
        gout_ref[...] += tn_dot(act_all[here], og_all[here])

    def pair(i):
        t = chunk(i)
        sib_copy(t).wait_recv()
        own[t] = (own[t].astype(F32) + sib_in[t].astype(F32)).astype(BF)

        @pl.when(t // Y != x)
        def _():
            a_copy(t).start()

        @pl.when(t % Y != y)
        def _():
            b_copy(t).start()

    def line(i):
        t = chunk(i)
        tx, ty = t // Y, t % Y

        @pl.when(tx == x)
        def _():
            total = own[t, low].astype(F32)
            for j in range(1, X):
                a_got(ty, x_peer(j)).wait_recv()
                total = total + rv_a[ty, x_peer(j)].astype(F32)
            st_a[ty] = total.astype(BF)

            @pl.when(ty != y)
            def _():
                fa_copy(ty).start()

        @pl.when(ty == y)
        def _():
            total = own[t, high].astype(F32)
            for j in range(1, Y):
                b_got(tx, y_peer(j)).wait_recv()
                total = total + rv_b[tx, y_peer(j)].astype(F32)
            st_b[tx] = total.astype(BF)

            @pl.when(tx != x)
            def _():
                fb_copy(tx).start()

    LAG1, LAG2 = 2, 4

    def del_step(i, _):
        @pl.when(i < NZ)
        def _():
            arrive(i)

        @pl.when((i >= LAG1) & (i < NZ + LAG1))
        def _():
            pair(i - LAG1)

        @pl.when(i >= LAG2)
        def _():
            line(i - LAG2)

        return 0

    lax.fori_loop(0, NZ + LAG2, del_step, 0)

    total = st_a[y].astype(F32)
    for j in range(1, Y):
        remote(fin_a.at[y_peer(j)], fin_a.at[y_peer(j)], fa_s.at[0], fa_r.at[y_peer(j)], sib).wait_recv()
        total = total + fin_a[y_peer(j)].astype(F32)
    ig_ref[low] = total.astype(BF)
    total = st_b[x].astype(F32)
    for j in range(1, X):
        remote(fin_b.at[x_peer(j)], fin_b.at[x_peer(j)], fb_s.at[0], fb_r.at[x_peer(j)], sib).wait_recv()
        total = total + fin_b[x_peer(j)].astype(F32)
    ig_ref[high] = total.astype(BF)

    og_ops[4]()
    in_ops[4]()

    def ring_sent(n, _):
        for sub in range(SUBS):
            ring_copy(act_all, sent_block(n), n, sub, act_s, act_r).wait_send()
            ring_copy(del_all, sent_block(n), n, sub, del_s, del_r).wait_send()
            rs_copy(n, sub).wait_send()
        return 0

    lax.fori_loop(0, MSGS, ring_sent, 0)

    def sum_sent(t, _):
        sib_copy(t).wait_send()

        @pl.when(t // Y != x)
        def _():
            a_copy(t).wait_send()

        @pl.when(t % Y != y)
        def _():
            b_copy(t).wait_send()

        return 0

    lax.fori_loop(0, X * Y, sum_sent, 0)
    for j in range(1, Y):
        fa_copy(y_peer(j)).wait_send()
    for j in range(1, X):
        fb_copy(x_peer(j)).wait_send()


def exchange(plan, og, inputs, preact, weight_in, weight_out):
    X, Y, NZ, TL, TB, DL, FL = plan.X, plan.Y, plan.nz, plan.TL, plan.TB, plan.DL, plan.FL
    nq, msgs = plan.nq, plan.msgs
    dma = pltpu.SemaphoreType.DMA
    vmem = pl.BlockSpec(memory_space=pltpu.VMEM)
    gather_sems = [
        dma((2, X - 1)),
        dma((X - 1, Y - 1)),
        dma((Y - 1, X - 1)),
        dma((nq,)),
        dma((nq,)),
        dma((nq,)),
        dma((nq,)),
    ]
    return pl.pallas_call(
        functools.partial(kernel, plan),
        out_shape=(
            jax.ShapeDtypeStruct((TL, DL), BF),
            jax.ShapeDtypeStruct((DL, FL), F32),
            jax.ShapeDtypeStruct((FL, DL), F32),
        ),
        in_specs=[vmem] * 5,
        out_specs=(vmem,) * 3,
        scratch_shapes=[
            pltpu.VMEM((nq * TB, DL), BF),
            pltpu.VMEM((nq * TB, DL), BF),
            pltpu.VMEM((NZ * TB, FL), BF),
            pltpu.VMEM((NZ * TB, FL), BF),
            pltpu.VMEM((TB, FL), F32),
            pltpu.VMEM((NZ + 1, TB, FL), BF),
            pltpu.VMEM((NZ, TL, DL), BF),
            pltpu.VMEM((NZ, TL, DL), BF),
            pltpu.VMEM((NZ, TL, DL), BF),
            pltpu.VMEM((Y, X, TL // 2, DL), BF),
            pltpu.VMEM((X, Y, TL // 2, DL), BF),
            pltpu.VMEM((Y, TL // 2, DL), BF),
            pltpu.VMEM((X, TL // 2, DL), BF),
            pltpu.VMEM((Y, TL // 2, DL), BF),
            pltpu.VMEM((X, TL // 2, DL), BF),
        ]
        + [dma((msgs, SUBS))] * 6
        + gather_sems * 2
        + [dma((nq,)), dma((nq,))]
        + [dma((nq,)), dma((Y, X)), dma((nq,)), dma((X, Y))]
        + [dma((Y,)), dma((Y,)), dma((X,)), dma((X,))],
        compiler_params=pltpu.CompilerParams(
            collective_id=0, has_side_effects=True, vmem_limit_bytes=40 * 1024 * 1024
        ),
    )(og, inputs, preact, weight_in, weight_out)


def shards(
    plan, inputs, out_grad, preact, weight_in, weight_out, moment_in, second_in, moment_out, second_out
):
    input_grad, grad_in, grad_out = exchange(plan, out_grad, inputs, preact, weight_in, weight_out)
    weight_a, moment_a, second_a = adam_step(weight_in, moment_in, second_in, grad_in)
    weight_b, moment_b, second_b = adam_step(weight_out, moment_out, second_out, grad_out)
    return (input_grad, weight_a, moment_a, second_a, weight_b, moment_b, second_b)


def solution(mesh):
    n_row, n_col = mesh.shape["row"], mesh.shape["col"]

    def whole(inputs, out_grad, preact, *rest):
        plan = Plan(
            n_row, n_col, inputs.shape[0] // n_row, inputs.shape[1] // n_col, preact.shape[1] // n_row
        )
        by_token, by_weight = P("row", "col"), P("col", "row")
        return jax.shard_map(
            functools.partial(shards, plan),
            mesh=mesh,
            in_specs=(
                by_token,
                by_token,
                by_weight,
                by_weight,
                by_token,
                by_weight,
                by_weight,
                by_token,
                by_token,
            ),
            out_specs=(by_token, by_weight, by_weight, by_weight, by_token, by_token, by_token),
            check_vma=False,
        )(inputs, out_grad, preact, *rest)

    return whole
```

```python
import functools
import math

import jax
import jax.numpy as jnp
from jax import lax
from jax.experimental import pallas as pl
from jax.experimental.pallas import tpu as pltpu
from jax.sharding import PartitionSpec as P

gelu_coef = 0.7978845608
beta_first = 0.9
beta_second = 0.95
learn_rate = 0.003
epsilon_adam = 1e-08
correct_first = 1.0 - 0.9**10
correct_second = 1.0 - 0.95**10

MESH = pl.DeviceIdType.MESH
BF = jnp.bfloat16
F32 = jnp.float32


def PEERS(n):
    return (1, n - 1) + tuple(range(2, n - 1)) if n > 2 else (1,)


def gelu_parts(preact):
    values = preact.astype(jnp.float32)
    tangent = jnp.tanh(gelu_coef * (values + 0.044715 * values * values * values))
    activated = 0.5 * values * (1.0 + tangent)
    slopes = 0.5 * (1.0 + tangent) + 0.5 * values * (1.0 - tangent * tangent) * gelu_coef * (
        1.0 + 3.0 * 0.044715 * values * values
    )
    return (activated, slopes)


def adam_step(weight, moment, second, grads):
    first_new = beta_first * moment.astype(jnp.float32) + (1.0 - beta_first) * grads
    second_new = beta_second * second.astype(jnp.float32) + (1.0 - beta_second) * grads * grads
    weight_new = weight.astype(jnp.float32) - learn_rate * (first_new / correct_first) / (
        jnp.sqrt(second_new / correct_second) + epsilon_adam
    )
    return (
        weight_new.astype(jnp.bfloat16),
        first_new.astype(jnp.bfloat16),
        second_new.astype(jnp.bfloat16),
    )


def nt_dot(left, right):
    return lax.dot_general(left, right, (((1,), (1,)), ((), ())), preferred_element_type=F32)


def tn_dot(left, right):
    return lax.dot_general(left, right, (((0,), (0,)), ((), ())), preferred_element_type=F32)


class Plan:
    def __init__(self, n_row, n_col, tokens, features, hidden):
        self.nq = n_row // 2
        self.X = math.isqrt(self.nq)
        self.Y = self.nq // self.X
        self.nz = n_col
        self.long = n_col // 2
        self.short = n_col - 1 - self.long
        self.msgs = n_col - 1
        self.TL = tokens
        self.TB = 2 * tokens
        self.DL = features
        self.FL = hidden
        self.subs_act, self.subs_rs, self.subs_del = 2, 4, 4
        self.act_1, self.act_2, self.act_3, self.act_every = 2, 2, 10, 2
        self.lag1, self.lag2 = 3, 7
        self.jump_rs, self.jump_del = 1, 1
        self.call = 0


def kernel(
    plan,
    og_ref,
    in_ref,
    pre_ref,
    win_ref,
    wout_ref,
    ig_ref,
    gin_ref,
    gout_ref,
    og_all,
    in_all,
    act_all,
    del_all,
    pre,
    win,
    wout,
    slopes,
    ring,
    sib_out,
    sib_in,
    own,
    rv_a,
    rv_b,
    st_a,
    st_b,
    fin_a,
    fin_b,
    load,
    sent,
    act_r,
    rs_r,
    del_r,
    og_a_r,
    og_b_r,
    og_sib_r,
    in_a_r,
    in_b_r,
    in_sib_r,
    sib_r,
    ra_r,
    rb_r,
    fa_r,
    fb_r,
):
    X, Y, NZ, TL, TB = plan.X, plan.Y, plan.nz, plan.TL, plan.TB
    HALF, MSGS = TL // 2, plan.msgs
    r = lax.axis_index("row")
    z = lax.axis_index("col")
    q = r // 2
    c = r % 2
    x = q // Y
    y = q % Y
    sgn = 1 - 2 * c
    sib = (r + sgn, z)
    OG, IN, ACT, RS, DEL, SIB, RA, RB, FA, FB = (sent.at[k] for k in range(10))

    def chip(cx, cy):
        return ((cx * Y + cy) * 2 + c, z)

    def x_peer(j):
        return (x + j) % X

    def y_peer(j):
        return (y + j) % Y

    def remote(src, dst, ssem, rsem, dev):
        return pltpu.make_async_remote_copy(
            src_ref=src, dst_ref=dst, send_sem=ssem, recv_sem=rsem, device_id=dev, device_id_type=MESH
        )

    def rows(buf, start, size):
        return buf.at[pl.ds(pl.multiple_of(start, 16), size)]

    def sign(n):
        return (1 - 2 * (n % 2)) * sgn

    def plane(step):
        return (r, (z + step + NZ) % NZ)

    def at_step(i, a):
        return (i + 32 - a) // 32 - (i + 31 - a) // 32

    class Ring:
        def __init__(self, buf, jump, subs, ssem, rsem):
            self.buf, self.jump, self.subs, self.ssem, self.rsem = buf, jump, subs, ssem, rsem

        def copy(self, block, n, sub, hops):
            size = TB // self.subs
            part = rows(self.buf, block * TB + sub * size, size)
            return remote(part, part, self.ssem, self.rsem.at[n, sub], plane(sign(n) * hops))

        def start(self):
            for dist in (1, self.jump) if self.jump > 1 else (1,):
                for n in (2 * dist - 2, 2 * dist - 1):
                    for sub in range(self.subs):
                        self.copy(z, n, sub, dist).start()

        def passed(self, n):
            block = (z - sign(n) * (n // 2 + 1) + 2 * NZ) % NZ
            for sub in range(self.subs):
                self.copy(block, n, sub, 1).wait_recv()

                @pl.when((n + 2 < MSGS) & (n // 2 + 2 != (self.jump if self.jump > 1 else 0)))
                def _():
                    self.copy(block, n + 2, sub, 1).start()

    acts = Ring(act_all, 1, plan.subs_act, ACT, act_r)
    deltas = Ring(del_all, plan.jump_del, plan.subs_del, DEL, del_r)

    def block_rows(buf, cx, cy, part=None, core=None):
        start = ((cx * Y + cy) * 2 + (c if core is None else core)) * TL
        if part is None:
            return rows(buf, start, TL)
        return rows(buf, start + part * HALF, HALF)

    class Gather:
        def __init__(self, buf, ssem, a_r, b_r, s_r):
            self.buf, self.ssem, self.a_r, self.b_r, self.s_r = buf, ssem, a_r, b_r, s_r

        def copy(self, cx, cy, part, sem, dev, core=None):
            ref = block_rows(self.buf, cx, cy, part, core)
            return remote(ref, ref, self.ssem, sem.at[cx * Y + cy], dev)

        def to_sib(self, cx, cy):
            return self.copy(cx, cy, None, self.s_r, sib)

        def from_sib(self, cx, cy):
            return self.copy(cx, cy, None, self.s_r, sib, 1 - c)

        def first(self):
            for j in PEERS(X):
                self.copy(x, y, None, self.a_r, chip(x_peer(j), y)).start()
            for j in PEERS(Y):
                self.copy(x, y, None, self.a_r, chip(x, y_peer(j))).start()
            self.to_sib(x, y).start()

        def second(self, j):
            self.copy(x_peer(j), y, None, self.a_r, sib).wait_recv()
            for k in PEERS(Y):
                self.copy(x_peer(j), y, 0, self.a_r, chip(x, y_peer(k))).start()
            self.copy(x, y_peer(j), None, self.a_r, sib).wait_recv()
            for k in PEERS(X):
                self.copy(x, y_peer(j), 1, self.b_r, chip(x_peer(k), y)).start()
            self.to_sib(x_peer(j), y).start()
            self.to_sib(x, y_peer(j)).start()

        def third(self, i):
            cx = x_peer(i // (Y - 1) + 1)
            cy = y_peer(i % (Y - 1) + 1)
            self.copy(cx, cy, 0, self.a_r, sib).wait_recv()
            self.copy(cx, cy, 1, self.b_r, sib).wait_recv()
            self.to_sib(cx, cy).start()

        def sent(self):
            size = (X + Y - 2) * TL + (X - 1) * (Y - 1) * 2 * HALF + X * Y * TL
            whole = rows(self.buf, 0, size)
            remote(whole, whole, self.ssem, self.s_r.at[0], sib).wait_send()

    THIRDS = (X - 1) * (Y - 1)
    og = Gather(og_all, OG, og_a_r, og_b_r, og_sib_r)
    inp = Gather(in_all, IN, in_a_r, in_b_r, in_sib_r)

    def loop(low, high, body):
        def step(i, _):
            body(i)
            return 0

        lax.fori_loop(low, high, step, 0)

    barrier = pltpu.get_barrier_semaphore()
    friends = [sib]
    for hops in sorted({1, plan.jump_rs, plan.jump_del}):
        friends += [plane(hops), plane(-hops)]
    friends += [chip(x_peer(j), y) for j in range(1, X)]
    friends += [chip(x, y_peer(j)) for j in range(1, Y)]
    for friend in friends:
        pl.semaphore_signal(barrier, inc=1, device_id=friend, device_id_type=MESH)
    get_pre = pltpu.make_async_copy(pre_ref, pre, load.at[0])
    get_og = pltpu.make_async_copy(og_ref, rows(og_all, r * TL, TL), load.at[1])
    get_wout = pltpu.make_async_copy(wout_ref, wout, load.at[2])
    get_in = pltpu.make_async_copy(in_ref, rows(in_all, r * TL, TL), load.at[3])
    get_win = pltpu.make_async_copy(win_ref, win, load.at[4])
    for get in (get_pre, get_og, get_wout, get_in, get_win):
        get.start()
    block = pl.ds(pl.multiple_of(z * TB, 16), TB)
    LONG, SHORT, JUMP = plan.long, plan.short, plan.jump_rs
    FAR, OWN = LONG + 1, LONG + 2
    fresh = [(0, LONG), (1, SHORT), (1, OWN)]
    if JUMP > 1:
        fresh += [(0, JUMP - 1), (1, JUMP - 1)]
    for way, slot in fresh:
        ring[way, slot] = jnp.zeros((TB, plan.FL), BF)
    gin_ref[...] = jnp.zeros_like(gin_ref)
    gout_ref[...] = jnp.zeros_like(gout_ref)
    get_pre.wait()
    act, slope = gelu_parts(pre[...])
    act_all[block] = act.astype(BF)
    slopes[...] = slope
    get_og.wait()
    pl.semaphore_wait(barrier, len(friends))

    og.first()
    acts.start()
    get_in.wait()
    get_wout.wait()
    get_win.wait()
    loop(1, X, og.second)
    loop(0, plan.act_1, acts.passed)
    loop(0, THIRDS, og.third)
    loop(plan.act_1, plan.act_2, acts.passed)
    inp.first()

    def rs_copy(way, dist, sub):
        size = TB // plan.subs_rs
        here = pl.ds(sub * size, size)
        direct = at_step(dist, JUMP)
        into = dist - 1 + direct * (FAR - JUMP + 1)
        hops = 1 + direct * (JUMP - 1)
        return remote(
            ring.at[way, dist, here],
            ring.at[way, into, here],
            RS,
            rs_r.at[way, into, sub],
            plane((1 - 2 * way) * sgn * hops),
        )

    def rs_got(way, slot, sub):
        size = TB // plan.subs_rs
        ref = ring.at[way, slot, pl.ds(sub * size, size)]
        return remote(ref, ref, RS, rs_r.at[way, slot, sub], sib)

    def rs_step(n):
        way = n % 2
        k = n // 2 + way
        dist = LONG - k
        if JUMP > 1:
            dist = dist - at_step(k, LONG - JUMP) + at_step(k, LONG - JUMP + 1)
        t = (z + (1 - 2 * way) * sgn * dist + NZ) % NZ
        og.from_sib(t // Y, t % Y).wait_recv()
        at = pl.multiple_of(t * TB, 16)
        part = nt_dot(og_all[pl.ds(at, TB)], wout[...]).astype(BF).astype(F32)
        size = TB // plan.subs_rs
        slot = dist + at_step(dist, 0) * OWN
        for sub in range(plan.subs_rs):
            here = pl.ds(sub * size, size)

            @pl.when((n >= 2) & (dist != (JUMP - 1 if JUMP > 1 else 0)) & (dist != 0))
            def _():
                rs_got(way, dist, sub).wait_recv()

            ring[way, slot, here] = (
                ring[way, slot, here].astype(F32) + part[sub * size : (sub + 1) * size]
            ).astype(BF)

            @pl.when(dist != 0)
            def _():
                rs_copy(way, dist, sub).start()

        m = plan.act_2 + n // plan.act_every

        @pl.when((n % plan.act_every == plan.act_every - 1) & (m < plan.act_3))
        def _():
            acts.passed(m)

        @pl.when((n >= 2) & (n < 1 + X))
        def _():
            inp.second(n - 1)

        @pl.when((n >= NZ - THIRDS))
        def _():
            inp.third(n - (NZ - THIRDS))

    loop(0, NZ, rs_step)
    total = ring[1, OWN].astype(F32)
    for slot in (0, FAR) if JUMP > 1 else (FAR,):
        for way in (0, 1):
            for sub in range(plan.subs_rs):
                rs_got(way, slot, sub).wait_recv()
            total = total + ring[way, slot].astype(F32)
    del_all[block] = (total * slopes[...]).astype(BF)
    deltas.start()
    loop(0, X * Y, lambda i: inp.from_sib(i // Y, i % Y).wait_recv())

    def far(i):
        k = (i + 1) // 2
        return k + at_step(k, 2) - at_step(k, 3) if plan.jump_del == 3 else k

    def message(i):
        return 2 * far(i) - 1 - i % 2

    def chunk(i):
        sig = (2 * (i % 2) - 1) * sgn
        return (z - sig * far(i) + 2 * NZ) % NZ

    def sib_copy(t):
        return remote(sib_out.at[t], sib_in.at[t], SIB, sib_r.at[t], sib)

    low, high = pl.ds(0, HALF), pl.ds(HALF, HALF)

    def a_copy(t):
        tx, ty = t // Y, t % Y
        return remote(own.at[t, low], rv_a.at[ty, x], RA, ra_r.at[ty, x], chip(tx, y))

    def a_got(ty, sx):
        return remote(rv_a.at[ty, sx], rv_a.at[ty, sx], RA, ra_r.at[ty, sx], sib)

    def b_copy(t):
        tx, ty = t // Y, t % Y
        return remote(own.at[t, high], rv_b.at[tx, y], RB, rb_r.at[tx, y], chip(x, ty))

    def b_got(tx, sy):
        return remote(rv_b.at[tx, sy], rv_b.at[tx, sy], RB, rb_r.at[tx, sy], sib)

    def fa_copy(ty):
        return remote(st_a.at[ty], fin_a.at[y], FA, fa_r.at[y], chip(x, ty))

    def fb_copy(tx):
        return remote(st_b.at[tx], fin_b.at[x], FB, fb_r.at[x], chip(tx, y))

    def arrive(i):
        @pl.when(i >= 1)
        def _():
            deltas.passed(message(i))

        t = chunk(i)
        at = pl.multiple_of(t * TB, 16)
        theirs = pl.ds(pl.multiple_of(at + (1 - c) * TL, 16), TL)
        sib_out[t] = nt_dot(del_all[theirs], win[...]).astype(BF)
        sib_copy(t).start()
        ours = pl.ds(pl.multiple_of(at + c * TL, 16), TL)
        own[t] = nt_dot(del_all[ours], win[...]).astype(BF)

        @pl.when((i >= plan.act_3 + 1) & (i < MSGS + 1))
        def _():
            acts.passed(i - 1)

        here = pl.ds(at, TB)
        gin_ref[...] += tn_dot(in_all[here], del_all[here])
        gout_ref[...] += tn_dot(act_all[here], og_all[here])

    def pair(i):
        t = chunk(i)
        sib_copy(t).wait_recv()
        own[t] = (own[t].astype(F32) + sib_in[t].astype(F32)).astype(BF)

        @pl.when(t // Y != x)
        def _():
            a_copy(t).start()

        @pl.when(t % Y != y)
        def _():
            b_copy(t).start()

    def line(i):
        t = chunk(i)
        tx, ty = t // Y, t % Y

        @pl.when(tx == x)
        def _():
            total = own[t, low].astype(F32)
            for j in range(1, X):
                a_got(ty, x_peer(j)).wait_recv()
                total = total + rv_a[ty, x_peer(j)].astype(F32)
            st_a[ty] = total.astype(BF)

            @pl.when(ty != y)
            def _():
                fa_copy(ty).start()

        @pl.when(ty == y)
        def _():
            total = own[t, high].astype(F32)
            for j in range(1, Y):
                b_got(tx, y_peer(j)).wait_recv()
                total = total + rv_b[tx, y_peer(j)].astype(F32)
            st_b[tx] = total.astype(BF)

            @pl.when(tx != x)
            def _():
                fb_copy(tx).start()

    LAG1, LAG2 = plan.lag1, plan.lag2

    def del_step(i):
        @pl.when(i < NZ)
        def _():
            arrive(i)

        @pl.when((i >= LAG1) & (i < NZ + LAG1))
        def _():
            pair(i - LAG1)

        @pl.when(i >= LAG2)
        def _():
            line(i - LAG2)

    loop(0, NZ + LAG2, del_step)

    og.sent()
    inp.sent()
    messages = rows(act_all, 0, MSGS * TB)
    remote(messages, messages, ACT, act_r.at[0, 0], sib).wait_send()
    remote(messages, messages, DEL, del_r.at[0, 0], sib).wait_send()
    remote(messages, messages, RS, act_r.at[0, 0], sib).wait_send()
    remote(sib_out, sib_out, SIB, sib_r.at[0], sib).wait_send()
    halves = sib_out.at[pl.ds(0, (X - 1) * Y // 2)]
    remote(halves, halves, RA, sib_r.at[0], sib).wait_send()
    halves = sib_out.at[pl.ds(0, (Y - 1) * X // 2)]
    remote(halves, halves, RB, sib_r.at[0], sib).wait_send()

    total = st_a[y].astype(F32)
    for j in range(1, Y):
        remote(fin_a.at[y_peer(j)], fin_a.at[y_peer(j)], FA, fa_r.at[y_peer(j)], sib).wait_recv()
        total = total + fin_a[y_peer(j)].astype(F32)
    ig_ref[low] = total.astype(BF)
    total = st_b[x].astype(F32)
    for j in range(1, X):
        remote(fin_b.at[x_peer(j)], fin_b.at[x_peer(j)], FB, fb_r.at[x_peer(j)], sib).wait_recv()
        total = total + fin_b[x_peer(j)].astype(F32)
    ig_ref[high] = total.astype(BF)
    last = st_a.at[pl.ds(0, Y - 1)]
    remote(last, last, FA, fa_r.at[0], sib).wait_send()
    last = st_b.at[pl.ds(0, X - 1)]
    remote(last, last, FB, fb_r.at[0], sib).wait_send()


def exchange(plan, og, inputs, preact, weight_in, weight_out):
    X, Y, NZ, TL, TB, DL, FL = plan.X, plan.Y, plan.nz, plan.TL, plan.TB, plan.DL, plan.FL
    nq, msgs = plan.nq, plan.msgs
    dma = pltpu.SemaphoreType.DMA
    vmem = pl.BlockSpec(memory_space=pltpu.VMEM)
    hbm = pl.BlockSpec(memory_space=pltpu.HBM)
    return pl.pallas_call(
        functools.partial(kernel, plan),
        out_shape=(
            jax.ShapeDtypeStruct((TL, DL), BF),
            jax.ShapeDtypeStruct((DL, FL), F32),
            jax.ShapeDtypeStruct((FL, DL), F32),
        ),
        in_specs=[hbm] * 5,
        out_specs=(vmem,) * 3,
        scratch_shapes=[
            pltpu.VMEM((nq * TB, DL), BF),
            pltpu.VMEM((nq * TB, DL), BF),
            pltpu.VMEM((NZ * TB, FL), BF),
            pltpu.VMEM((NZ * TB, FL), BF),
            pltpu.VMEM((TB, FL), BF),
            pltpu.VMEM((DL, FL), BF),
            pltpu.VMEM((FL, DL), BF),
            pltpu.VMEM((TB, FL), F32),
            pltpu.VMEM((2, plan.long + 3, TB, FL), BF),
            pltpu.VMEM((NZ, TL, DL), BF),
            pltpu.VMEM((NZ, TL, DL), BF),
            pltpu.VMEM((NZ, TL, DL), BF),
            pltpu.VMEM((Y, X, TL // 2, DL), BF),
            pltpu.VMEM((X, Y, TL // 2, DL), BF),
            pltpu.VMEM((Y, TL // 2, DL), BF),
            pltpu.VMEM((X, TL // 2, DL), BF),
            pltpu.VMEM((Y, TL // 2, DL), BF),
            pltpu.VMEM((X, TL // 2, DL), BF),
            dma((5,)),
            dma((10,)),
            dma((msgs, plan.subs_act)),
            dma((2, plan.long + 2, plan.subs_rs)),
            dma((msgs, plan.subs_del)),
        ]
        + [dma((nq,))] * 7
        + [dma((Y, X)), dma((X, Y)), dma((Y,)), dma((X,))],
        compiler_params=pltpu.CompilerParams(
            collective_id=plan.call, has_side_effects=True, vmem_limit_bytes=40 * 1024 * 1024
        ),
    )(og, inputs, preact, weight_in, weight_out)


def shards(
    plan, inputs, out_grad, preact, weight_in, weight_out, moment_in, second_in, moment_out, second_out
):
    input_grad, grad_in, grad_out = exchange(plan, out_grad, inputs, preact, weight_in, weight_out)
    weight_a, moment_a, second_a = adam_step(weight_in, moment_in, second_in, grad_in)
    weight_b, moment_b, second_b = adam_step(weight_out, moment_out, second_out, grad_out)
    return (input_grad, weight_a, moment_a, second_a, weight_b, moment_b, second_b)


def solution(mesh):
    n_row, n_col = mesh.shape["row"], mesh.shape["col"]

    def whole(inputs, out_grad, preact, *rest):
        plan = Plan(
            n_row, n_col, inputs.shape[0] // n_row, inputs.shape[1] // n_col, preact.shape[1] // n_row
        )
        by_token, by_weight = P("row", "col"), P("col", "row")
        return jax.shard_map(
            functools.partial(shards, plan),
            mesh=mesh,
            in_specs=(
                by_token,
                by_token,
                by_weight,
                by_weight,
                by_token,
                by_weight,
                by_weight,
                by_token,
                by_token,
            ),
            out_specs=(by_token, by_weight, by_weight, by_weight, by_token, by_token, by_token),
            check_vma=False,
        )(inputs, out_grad, preact, *rest)

    return whole
```

```python
import functools
import math

import jax
import jax.numpy as jnp
from jax import lax
from jax.experimental import pallas as pl
from jax.experimental.pallas import tpu as pltpu
from jax.sharding import PartitionSpec as P

gelu_coef = 0.7978845608
beta_first = 0.9
beta_second = 0.95
learn_rate = 0.003
epsilon_adam = 1e-08
correct_first = 1.0 - 0.9**10
correct_second = 1.0 - 0.95**10

MESH = pl.DeviceIdType.MESH
BF = jnp.bfloat16
F32 = jnp.float32


def PEERS(n):
    return (1, n - 1) + tuple(range(2, n - 1)) if n > 2 else (1,)


def gelu_parts(preact):
    values = preact.astype(jnp.float32)
    tangent = jnp.tanh(gelu_coef * (values + 0.044715 * values * values * values))
    activated = 0.5 * values * (1.0 + tangent)
    slopes = 0.5 * (1.0 + tangent) + 0.5 * values * (1.0 - tangent * tangent) * gelu_coef * (
        1.0 + 3.0 * 0.044715 * values * values
    )
    return (activated, slopes)


def adam_step(weight, moment, second, grads):
    first_new = beta_first * moment.astype(jnp.float32) + (1.0 - beta_first) * grads
    second_new = beta_second * second.astype(jnp.float32) + (1.0 - beta_second) * grads * grads
    weight_new = weight.astype(jnp.float32) - learn_rate * (first_new / correct_first) / (
        jnp.sqrt(second_new / correct_second) + epsilon_adam
    )
    return (
        weight_new.astype(jnp.bfloat16),
        first_new.astype(jnp.bfloat16),
        second_new.astype(jnp.bfloat16),
    )


def nt_dot(left, right):
    return lax.dot_general(left, right, (((1,), (1,)), ((), ())), preferred_element_type=F32)


def tn_dot(left, right):
    return lax.dot_general(left, right, (((0,), (0,)), ((), ())), preferred_element_type=F32)


class Plan:
    def __init__(self, n_row, n_col, tokens, features, hidden):
        self.nq = n_row // 2
        self.X = math.isqrt(self.nq)
        self.Y = self.nq // self.X
        self.nz = n_col
        self.long = n_col // 2
        self.short = n_col - 1 - self.long
        self.msgs = n_col - 1
        self.TL = tokens
        self.TB = 2 * tokens
        self.DL = features
        self.FL = hidden
        self.subs_act, self.subs_rs, self.subs_del = 2, 4, 4
        self.act_1, self.act_2, self.act_3, self.act_every = 2, 2, 10, 2
        self.lag1, self.lag2 = 3, 7
        self.jump_rs, self.jump_del = 1, 1
        self.lead, self.in_1 = 4, 2
        self.ops = 2
        self.call = 0


def kernel(
    plan,
    og_ref,
    in_ref,
    pre_ref,
    win_ref,
    wout_ref,
    ig_ref,
    gin_ref,
    gout_ref,
    og_all,
    in_all,
    act_all,
    del_all,
    pre,
    win,
    wout,
    slopes,
    ring,
    sib_out,
    sib_in,
    own,
    rv_a,
    rv_b,
    st_a,
    st_b,
    fin_a,
    fin_b,
    load,
    sent,
    act_r,
    rs_r,
    del_r,
    og_a_r,
    og_b_r,
    og_sib_r,
    in_a_r,
    in_b_r,
    in_sib_r,
    sib_r,
    ra_r,
    rb_r,
    fa_r,
    fb_r,
):
    X, Y, NZ, TL, TB = plan.X, plan.Y, plan.nz, plan.TL, plan.TB
    HALF, MSGS = TL // 2, plan.msgs
    r = lax.axis_index("row")
    z = lax.axis_index("col")

    def div(a, n):
        if isinstance(a, int):
            return a // n
        if plan.ops == 2 and n & (n - 1) == 0:
            return lax.shift_right_logical(a, jnp.int32(n.bit_length() - 1))
        return lax.div(a, jnp.int32(n)) if plan.ops else a // n

    def mod(a, n):
        if isinstance(a, int):
            return a % n
        if plan.ops == 2 and n & (n - 1) == 0:
            return a & (n - 1)
        return lax.rem(a, jnp.int32(n)) if plan.ops else a % n

    q = div(r, 2)
    c = mod(r, 2)
    x = div(q, Y)
    y = mod(q, Y)
    sgn = 1 - 2 * c
    sib = (r + sgn, z)
    OG, IN, ACT, RS, DEL, SIB, RA, RB, FA, FB = (sent.at[k] for k in range(10))

    def chip(cx, cy):
        return ((cx * Y + cy) * 2 + c, z)

    def x_peer(j):
        return mod(x + j, X)

    def y_peer(j):
        return mod(y + j, Y)

    def remote(src, dst, ssem, rsem, dev):
        return pltpu.make_async_remote_copy(
            src_ref=src, dst_ref=dst, send_sem=ssem, recv_sem=rsem, device_id=dev, device_id_type=MESH
        )

    def rows(buf, start, size):
        return buf.at[pl.ds(pl.multiple_of(start, 16), size)]

    def sign(n):
        return (1 - 2 * mod(n, 2)) * sgn

    def plane(step):
        return (r, mod(z + step + NZ, NZ))

    def at_step(i, a):
        return jnp.where(i == a, 1, 0)

    class Ring:
        def __init__(self, buf, jump, subs, ssem, rsem):
            self.buf, self.jump, self.subs, self.ssem, self.rsem = buf, jump, subs, ssem, rsem

        def copy(self, block, n, sub, hops):
            size = TB // self.subs
            part = rows(self.buf, block * TB + sub * size, size)
            return remote(part, part, self.ssem, self.rsem.at[n, sub], plane(sign(n) * hops))

        def start(self):
            for dist in (1, self.jump) if self.jump > 1 else (1,):
                for n in (2 * dist - 2, 2 * dist - 1):
                    for sub in range(self.subs):
                        self.copy(z, n, sub, dist).start()

        def passed(self, n):
            block = mod(z - sign(n) * (div(n, 2) + 1) + 2 * NZ, NZ)
            for sub in range(self.subs):
                self.copy(block, n, sub, 1).wait_recv()

                @pl.when((n + 2 < MSGS) & (div(n, 2) + 2 != (self.jump if self.jump > 1 else 0)))
                def _():
                    self.copy(block, n + 2, sub, 1).start()

    acts = Ring(act_all, 1, plan.subs_act, ACT, act_r)
    deltas = Ring(del_all, plan.jump_del, plan.subs_del, DEL, del_r)

    def block_rows(buf, cx, cy, part=None, core=None):
        start = ((cx * Y + cy) * 2 + (c if core is None else core)) * TL
        if part is None:
            return rows(buf, start, TL)
        return rows(buf, start + part * HALF, HALF)

    class Gather:
        def __init__(self, buf, ssem, a_r, b_r, s_r):
            self.buf, self.ssem, self.a_r, self.b_r, self.s_r = buf, ssem, a_r, b_r, s_r

        def copy(self, cx, cy, part, sem, dev, core=None):
            ref = block_rows(self.buf, cx, cy, part, core)
            return remote(ref, ref, self.ssem, sem.at[cx * Y + cy], dev)

        def to_sib(self, cx, cy):
            return self.copy(cx, cy, None, self.s_r, sib)

        def from_sib(self, cx, cy):
            return self.copy(cx, cy, None, self.s_r, sib, 1 - c)

        def first(self):
            for j in PEERS(X):
                self.copy(x, y, None, self.a_r, chip(x_peer(j), y)).start()
            for j in PEERS(Y):
                self.copy(x, y, None, self.a_r, chip(x, y_peer(j))).start()
            self.to_sib(x, y).start()

        def second_a(self, cx):
            self.copy(cx, y, None, self.a_r, sib).wait_recv()
            for k in PEERS(Y):
                self.copy(cx, y, 0, self.a_r, chip(x, y_peer(k))).start()
            self.to_sib(cx, y).start()

        def second_b(self, cy):
            self.copy(x, cy, None, self.a_r, sib).wait_recv()
            for k in PEERS(X):
                self.copy(x, cy, 1, self.b_r, chip(x_peer(k), y)).start()
            self.to_sib(x, cy).start()

        def third(self, cx, cy):
            self.copy(cx, cy, 0, self.a_r, sib).wait_recv()
            self.copy(cx, cy, 1, self.b_r, sib).wait_recv()
            self.to_sib(cx, cy).start()

        def sent(self):
            size = (X + Y - 2) * TL + (X - 1) * (Y - 1) * 2 * HALF + X * Y * TL
            whole = rows(self.buf, 0, size)
            remote(whole, whole, self.ssem, self.s_r.at[0], sib).wait_send()

    THIRDS = (X - 1) * (Y - 1)
    og = Gather(og_all, OG, og_a_r, og_b_r, og_sib_r)
    inp = Gather(in_all, IN, in_a_r, in_b_r, in_sib_r)

    def loop(low, high, body):
        def step(i, _):
            body(i)
            return 0

        lax.fori_loop(low, high, step, 0)

    barrier = pltpu.get_barrier_semaphore()
    friends = [sib]
    for hops in sorted({1, plan.jump_rs, plan.jump_del}):
        friends += [plane(hops), plane(-hops)]
    friends += [chip(x_peer(j), y) for j in range(1, X)]
    friends += [chip(x, y_peer(j)) for j in range(1, Y)]
    for friend in friends:
        pl.semaphore_signal(barrier, inc=1, device_id=friend, device_id_type=MESH)
    get_pre = pltpu.make_async_copy(pre_ref, pre, load.at[0])
    get_og = pltpu.make_async_copy(og_ref, rows(og_all, r * TL, TL), load.at[1])
    get_wout = pltpu.make_async_copy(wout_ref, wout, load.at[2])
    get_in = pltpu.make_async_copy(in_ref, rows(in_all, r * TL, TL), load.at[3])
    get_win = pltpu.make_async_copy(win_ref, win, load.at[4])
    for get in (get_pre, get_og, get_wout, get_in, get_win):
        get.start()
    block = pl.ds(pl.multiple_of(z * TB, 16), TB)
    LONG, SHORT, JUMP = plan.long, plan.short, plan.jump_rs
    FAR, OWN = LONG + 1, LONG + 2
    fresh = [(0, LONG), (1, SHORT), (1, OWN)]
    if JUMP > 1:
        fresh += [(0, JUMP - 1), (1, JUMP - 1)]
    for way, slot in fresh:
        ring[way, slot] = jnp.zeros((TB, plan.FL), BF)
    gin_ref[...] = jnp.zeros_like(gin_ref)
    gout_ref[...] = jnp.zeros_like(gout_ref)
    get_og.wait()
    pl.semaphore_wait(barrier, len(friends))

    og.first()
    get_pre.wait()
    act, slope = gelu_parts(pre[...])
    act_all[block] = act.astype(BF)
    acts.start()
    slopes[...] = slope
    get_in.wait()
    get_wout.wait()
    get_win.wait()

    def needed(n):
        way = mod(n, 2)
        k = div(n, 2) + way
        dist = LONG - k
        if JUMP > 1:
            dist = dist - at_step(k, LONG - JUMP) + at_step(k, LONG - JUMP + 1)
        return way, dist, mod(z + (1 - 2 * way) * sgn * dist + NZ, NZ)

    def og_near(n):
        t = needed(n)[2]
        tx, ty = div(t, Y), mod(t, Y)

        @pl.when((tx != x) & (ty == y))
        def _():
            og.second_a(tx)

        @pl.when((tx == x) & (ty != y))
        def _():
            og.second_b(ty)

    def og_far(n):
        t = needed(n)[2]
        tx, ty = div(t, Y), mod(t, Y)

        @pl.when((tx != x) & (ty != y))
        def _():
            og.third(tx, ty)

    LEAD = plan.lead
    loop(0, NZ, og_near)
    loop(0, plan.act_1, acts.passed)
    loop(0, LEAD, og_far)
    loop(plan.act_1, plan.act_2, acts.passed)

    def rs_copy(way, dist, sub):
        size = TB // plan.subs_rs
        here = pl.ds(sub * size, size)
        direct = at_step(dist, JUMP)
        into = dist - 1 + direct * (FAR - JUMP + 1)
        hops = 1 + direct * (JUMP - 1)
        return remote(
            ring.at[way, dist, here],
            ring.at[way, into, here],
            RS,
            rs_r.at[way, into, sub],
            plane((1 - 2 * way) * sgn * hops),
        )

    def rs_got(way, slot, sub):
        size = TB // plan.subs_rs
        ref = ring.at[way, slot, pl.ds(sub * size, size)]
        return remote(ref, ref, RS, rs_r.at[way, slot, sub], sib)

    def rs_step(n):
        way, dist, t = needed(n)

        @pl.when(n + LEAD < NZ)
        def _():
            og_far(n + LEAD)

        og.from_sib(div(t, Y), mod(t, Y)).wait_recv()
        at = pl.multiple_of(t * TB, 16)
        part = nt_dot(og_all[pl.ds(at, TB)], wout[...]).astype(BF).astype(F32)
        size = TB // plan.subs_rs
        slot = jnp.where(dist == 0, OWN, dist)
        for sub in range(plan.subs_rs):
            here = pl.ds(sub * size, size)

            @pl.when((n >= 2) & (dist != (JUMP - 1 if JUMP > 1 else 0)) & (dist != 0))
            def _():
                rs_got(way, dist, sub).wait_recv()

            ring[way, slot, here] = (
                ring[way, slot, here].astype(F32) + part[sub * size : (sub + 1) * size]
            ).astype(BF)

            @pl.when(dist != 0)
            def _():
                rs_copy(way, dist, sub).start()

        m = plan.act_2 + div(n, plan.act_every)

        @pl.when((mod(n, plan.act_every) == plan.act_every - 1) & (m < plan.act_3))
        def _():
            acts.passed(m)

        @pl.when(n == plan.in_1)
        def _():
            inp.first()

        @pl.when((n > NZ - THIRDS - X) & (n < NZ - THIRDS))
        def _():
            j = n - (NZ - THIRDS - X)
            inp.second_a(x_peer(j))
            inp.second_b(y_peer(j))

        @pl.when((n >= NZ - THIRDS))
        def _():
            i = n - (NZ - THIRDS)
            inp.third(x_peer(div(i, Y - 1) + 1), y_peer(mod(i, Y - 1) + 1))

    loop(0, NZ, rs_step)
    total = ring[1, OWN].astype(F32)
    for slot in (0, FAR) if JUMP > 1 else (FAR,):
        for way in (0, 1):
            for sub in range(plan.subs_rs):
                rs_got(way, slot, sub).wait_recv()
            total = total + ring[way, slot].astype(F32)
    del_all[block] = (total * slopes[...]).astype(BF)
    deltas.start()
    loop(0, X * Y, lambda i: inp.from_sib(div(i, Y), mod(i, Y)).wait_recv())

    def far(i):
        k = div(i + 1, 2)
        return k + at_step(k, 2) - at_step(k, 3) if plan.jump_del == 3 else k

    def message(i):
        return 2 * far(i) - 1 - mod(i, 2)

    def chunk(i):
        sig = (2 * mod(i, 2) - 1) * sgn
        return mod(z - sig * far(i) + 2 * NZ, NZ)

    def sib_copy(t):
        return remote(sib_out.at[t], sib_in.at[t], SIB, sib_r.at[t], sib)

    low, high = pl.ds(0, HALF), pl.ds(HALF, HALF)

    def a_copy(t):
        tx, ty = div(t, Y), mod(t, Y)
        return remote(own.at[t, low], rv_a.at[ty, x], RA, ra_r.at[ty, x], chip(tx, y))

    def a_got(ty, sx):
        return remote(rv_a.at[ty, sx], rv_a.at[ty, sx], RA, ra_r.at[ty, sx], sib)

    def b_copy(t):
        tx, ty = div(t, Y), mod(t, Y)
        return remote(own.at[t, high], rv_b.at[tx, y], RB, rb_r.at[tx, y], chip(x, ty))

    def b_got(tx, sy):
        return remote(rv_b.at[tx, sy], rv_b.at[tx, sy], RB, rb_r.at[tx, sy], sib)

    def fa_copy(ty):
        return remote(st_a.at[ty], fin_a.at[y], FA, fa_r.at[y], chip(x, ty))

    def fb_copy(tx):
        return remote(st_b.at[tx], fin_b.at[x], FB, fb_r.at[x], chip(tx, y))

    def arrive(i):
        @pl.when(i >= 1)
        def _():
            deltas.passed(message(i))

        t = chunk(i)
        at = pl.multiple_of(t * TB, 16)
        theirs = pl.ds(pl.multiple_of(at + (1 - c) * TL, 16), TL)
        sib_out[t] = nt_dot(del_all[theirs], win[...]).astype(BF)
        sib_copy(t).start()
        ours = pl.ds(pl.multiple_of(at + c * TL, 16), TL)
        own[t] = nt_dot(del_all[ours], win[...]).astype(BF)

        @pl.when((i >= plan.act_3 + 1) & (i < MSGS + 1))
        def _():
            acts.passed(i - 1)

        here = pl.ds(at, TB)
        gin_ref[...] += tn_dot(in_all[here], del_all[here])
        gout_ref[...] += tn_dot(act_all[here], og_all[here])

    def pair(i):
        t = chunk(i)
        sib_copy(t).wait_recv()
        own[t] = (own[t].astype(F32) + sib_in[t].astype(F32)).astype(BF)

        @pl.when(div(t, Y) != x)
        def _():
            a_copy(t).start()

        @pl.when(mod(t, Y) != y)
        def _():
            b_copy(t).start()

    def line(i):
        t = chunk(i)
        tx, ty = div(t, Y), mod(t, Y)

        @pl.when(tx == x)
        def _():
            total = own[t, low].astype(F32)
            for j in range(1, X):
                a_got(ty, x_peer(j)).wait_recv()
                total = total + rv_a[ty, x_peer(j)].astype(F32)
            st_a[ty] = total.astype(BF)

            @pl.when(ty != y)
            def _():
                fa_copy(ty).start()

        @pl.when(ty == y)
        def _():
            total = own[t, high].astype(F32)
            for j in range(1, Y):
                b_got(tx, y_peer(j)).wait_recv()
                total = total + rv_b[tx, y_peer(j)].astype(F32)
            st_b[tx] = total.astype(BF)

            @pl.when(tx != x)
            def _():
                fb_copy(tx).start()

    LAG1, LAG2 = plan.lag1, plan.lag2

    def del_step(i):
        @pl.when(i < NZ)
        def _():
            arrive(i)

        @pl.when((i >= LAG1) & (i < NZ + LAG1))
        def _():
            pair(i - LAG1)

        @pl.when(i >= LAG2)
        def _():
            line(i - LAG2)

    loop(0, NZ + LAG2, del_step)

    og.sent()
    inp.sent()
    messages = rows(act_all, 0, MSGS * TB)
    remote(messages, messages, ACT, act_r.at[0, 0], sib).wait_send()
    remote(messages, messages, DEL, del_r.at[0, 0], sib).wait_send()
    remote(messages, messages, RS, act_r.at[0, 0], sib).wait_send()
    remote(sib_out, sib_out, SIB, sib_r.at[0], sib).wait_send()
    halves = sib_out.at[pl.ds(0, (X - 1) * Y // 2)]
    remote(halves, halves, RA, sib_r.at[0], sib).wait_send()
    halves = sib_out.at[pl.ds(0, (Y - 1) * X // 2)]
    remote(halves, halves, RB, sib_r.at[0], sib).wait_send()

    total = st_a[y].astype(F32)
    for j in range(1, Y):
        remote(fin_a.at[y_peer(j)], fin_a.at[y_peer(j)], FA, fa_r.at[y_peer(j)], sib).wait_recv()
        total = total + fin_a[y_peer(j)].astype(F32)
    ig_ref[low] = total.astype(BF)
    total = st_b[x].astype(F32)
    for j in range(1, X):
        remote(fin_b.at[x_peer(j)], fin_b.at[x_peer(j)], FB, fb_r.at[x_peer(j)], sib).wait_recv()
        total = total + fin_b[x_peer(j)].astype(F32)
    ig_ref[high] = total.astype(BF)
    last = st_a.at[pl.ds(0, Y - 1)]
    remote(last, last, FA, fa_r.at[0], sib).wait_send()
    last = st_b.at[pl.ds(0, X - 1)]
    remote(last, last, FB, fb_r.at[0], sib).wait_send()


def exchange(plan, og, inputs, preact, weight_in, weight_out):
    X, Y, NZ, TL, TB, DL, FL = plan.X, plan.Y, plan.nz, plan.TL, plan.TB, plan.DL, plan.FL
    nq, msgs = plan.nq, plan.msgs
    dma = pltpu.SemaphoreType.DMA
    vmem = pl.BlockSpec(memory_space=pltpu.VMEM)
    hbm = pl.BlockSpec(memory_space=pltpu.HBM)
    return pl.pallas_call(
        functools.partial(kernel, plan),
        out_shape=(
            jax.ShapeDtypeStruct((TL, DL), BF),
            jax.ShapeDtypeStruct((DL, FL), F32),
            jax.ShapeDtypeStruct((FL, DL), F32),
        ),
        in_specs=[hbm] * 5,
        out_specs=(vmem,) * 3,
        scratch_shapes=[
            pltpu.VMEM((nq * TB, DL), BF),
            pltpu.VMEM((nq * TB, DL), BF),
            pltpu.VMEM((NZ * TB, FL), BF),
            pltpu.VMEM((NZ * TB, FL), BF),
            pltpu.VMEM((TB, FL), BF),
            pltpu.VMEM((DL, FL), BF),
            pltpu.VMEM((FL, DL), BF),
            pltpu.VMEM((TB, FL), F32),
            pltpu.VMEM((2, plan.long + 3, TB, FL), BF),
            pltpu.VMEM((NZ, TL, DL), BF),
            pltpu.VMEM((NZ, TL, DL), BF),
            pltpu.VMEM((NZ, TL, DL), BF),
            pltpu.VMEM((Y, X, TL // 2, DL), BF),
            pltpu.VMEM((X, Y, TL // 2, DL), BF),
            pltpu.VMEM((Y, TL // 2, DL), BF),
            pltpu.VMEM((X, TL // 2, DL), BF),
            pltpu.VMEM((Y, TL // 2, DL), BF),
            pltpu.VMEM((X, TL // 2, DL), BF),
            dma((5,)),
            dma((10,)),
            dma((msgs, plan.subs_act)),
            dma((2, plan.long + 2, plan.subs_rs)),
            dma((msgs, plan.subs_del)),
        ]
        + [dma((nq,))] * 7
        + [dma((Y, X)), dma((X, Y)), dma((Y,)), dma((X,))],
        compiler_params=pltpu.CompilerParams(
            collective_id=plan.call, has_side_effects=True, vmem_limit_bytes=60 * 1024 * 1024
        ),
    )(og, inputs, preact, weight_in, weight_out)


def shards(
    plan, inputs, out_grad, preact, weight_in, weight_out, moment_in, second_in, moment_out, second_out
):
    input_grad, grad_in, grad_out = exchange(plan, out_grad, inputs, preact, weight_in, weight_out)
    weight_a, moment_a, second_a = adam_step(weight_in, moment_in, second_in, grad_in)
    weight_b, moment_b, second_b = adam_step(weight_out, moment_out, second_out, grad_out)
    return (input_grad, weight_a, moment_a, second_a, weight_b, moment_b, second_b)


def solution(mesh):
    n_row, n_col = mesh.shape["row"], mesh.shape["col"]

    def whole(inputs, out_grad, preact, *rest):
        plan = Plan(
            n_row, n_col, inputs.shape[0] // n_row, inputs.shape[1] // n_col, preact.shape[1] // n_row
        )
        by_token, by_weight = P("row", "col"), P("col", "row")
        return jax.shard_map(
            functools.partial(shards, plan),
            mesh=mesh,
            in_specs=(
                by_token,
                by_token,
                by_weight,
                by_weight,
                by_token,
                by_weight,
                by_weight,
                by_token,
                by_token,
            ),
            out_specs=(by_token, by_weight, by_weight, by_weight, by_token, by_token, by_token),
            check_vma=False,
        )(inputs, out_grad, preact, *rest)

    return whole
```

```python
import functools
import math

import jax
import jax.numpy as jnp
from jax import lax
from jax.experimental import pallas as pl
from jax.experimental.pallas import tpu as pltpu
from jax.sharding import PartitionSpec as P

gelu_coef = 0.7978845608
beta_first = 0.9
beta_second = 0.95
learn_rate = 0.003
epsilon_adam = 1e-08
correct_first = 1.0 - 0.9**10
correct_second = 1.0 - 0.95**10

MESH = pl.DeviceIdType.MESH
BF = jnp.bfloat16
F32 = jnp.float32


def PEERS(n):
    return (1, n - 1) + tuple(range(2, n - 1)) if n > 2 else (1,)


def gelu_parts(preact):
    values = preact.astype(jnp.float32)
    tangent = jnp.tanh(gelu_coef * (values + 0.044715 * values * values * values))
    activated = 0.5 * values * (1.0 + tangent)
    slopes = 0.5 * (1.0 + tangent) + 0.5 * values * (1.0 - tangent * tangent) * gelu_coef * (
        1.0 + 3.0 * 0.044715 * values * values
    )
    return (activated, slopes)


def adam_step(weight, moment, second, grads):
    first_new = beta_first * moment.astype(jnp.float32) + (1.0 - beta_first) * grads
    second_new = beta_second * second.astype(jnp.float32) + (1.0 - beta_second) * grads * grads
    weight_new = weight.astype(jnp.float32) - learn_rate * (first_new / correct_first) / (
        jnp.sqrt(second_new / correct_second) + epsilon_adam
    )
    return (
        weight_new.astype(jnp.bfloat16),
        first_new.astype(jnp.bfloat16),
        second_new.astype(jnp.bfloat16),
    )


def nt_dot(left, right):
    return lax.dot_general(left, right, (((1,), (1,)), ((), ())), preferred_element_type=F32)


def tn_dot(left, right):
    return lax.dot_general(left, right, (((0,), (0,)), ((), ())), preferred_element_type=F32)


class Plan:
    def __init__(self, n_row, n_col, tokens, features, hidden):
        self.nq = n_row // 2
        self.X = math.isqrt(self.nq)
        self.Y = self.nq // self.X
        self.nz = n_col
        self.long = n_col // 2
        self.short = n_col - 1 - self.long
        self.msgs = n_col - 1
        self.TL = tokens
        self.TB = 2 * tokens
        self.DL = features
        self.FL = hidden
        self.subs_act, self.subs_rs, self.subs_del = 2, 4, 4
        self.act_1, self.act_2, self.act_3, self.act_every = 2, 2, 10, 2
        self.lag1, self.lag2 = 3, 7
        self.jump_rs, self.jump_del = 1, 1
        self.lead, self.in_1, self.early, self.act_4 = 4, 2, 5, 11
        self.adam_rows = 32
        self.ops = 2
        self.call = 0


def kernel(
    plan,
    og_ref,
    in_ref,
    pre_ref,
    win_ref,
    wout_ref,
    moment_in_ref,
    second_in_ref,
    moment_out_ref,
    second_out_ref,
    ig_ref,
    new_win_ref,
    new_moment_in_ref,
    new_second_in_ref,
    new_wout_ref,
    new_moment_out_ref,
    new_second_out_ref,
    og_all,
    in_all,
    act_all,
    del_all,
    pre,
    win,
    wout,
    moments_in,
    seconds_in,
    moments_out,
    seconds_out,
    gin_ref,
    gout_ref,
    slopes,
    ring,
    sib_out,
    sib_in,
    own,
    rv_a,
    rv_b,
    st_a,
    st_b,
    fin_a,
    fin_b,
    load,
    sent,
    act_r,
    rs_r,
    del_r,
    og_a_r,
    og_b_r,
    og_sib_r,
    in_a_r,
    in_b_r,
    in_sib_r,
    sib_r,
    ra_r,
    rb_r,
    fa_r,
    fb_r,
):
    X, Y, NZ, TL, TB = plan.X, plan.Y, plan.nz, plan.TL, plan.TB
    HALF, MSGS = TL // 2, plan.msgs
    r = lax.axis_index("row")
    z = lax.axis_index("col")

    def div(a, n):
        if isinstance(a, int):
            return a // n
        if plan.ops == 2 and n & (n - 1) == 0:
            return lax.shift_right_logical(a, jnp.int32(n.bit_length() - 1))
        return lax.div(a, jnp.int32(n)) if plan.ops else a // n

    def mod(a, n):
        if isinstance(a, int):
            return a % n
        if plan.ops == 2 and n & (n - 1) == 0:
            return a & (n - 1)
        return lax.rem(a, jnp.int32(n)) if plan.ops else a % n

    q = div(r, 2)
    c = mod(r, 2)
    x = div(q, Y)
    y = mod(q, Y)
    sgn = 1 - 2 * c
    sib = (r + sgn, z)
    OG, IN, ACT, RS, DEL, SIB, RA, RB, FA, FB = (sent.at[k] for k in range(10))

    def chip(cx, cy):
        return ((cx * Y + cy) * 2 + c, z)

    def x_peer(j):
        return mod(x + j, X)

    def y_peer(j):
        return mod(y + j, Y)

    def remote(src, dst, ssem, rsem, dev):
        return pltpu.make_async_remote_copy(
            src_ref=src, dst_ref=dst, send_sem=ssem, recv_sem=rsem, device_id=dev, device_id_type=MESH
        )

    def rows(buf, start, size):
        return buf.at[pl.ds(pl.multiple_of(start, 16), size)]

    def sign(n):
        return (1 - 2 * mod(n, 2)) * sgn

    def plane(step):
        return (r, mod(z + step + NZ, NZ))

    def at_step(i, a):
        return jnp.where(i == a, 1, 0)

    class Ring:
        def __init__(self, buf, jump, subs, ssem, rsem):
            self.buf, self.jump, self.subs, self.ssem, self.rsem = buf, jump, subs, ssem, rsem

        def copy(self, block, n, sub, hops):
            size = TB // self.subs
            part = rows(self.buf, block * TB + sub * size, size)
            return remote(part, part, self.ssem, self.rsem.at[n, sub], plane(sign(n) * hops))

        def start(self):
            for dist in (1, self.jump) if self.jump > 1 else (1,):
                for n in (2 * dist - 2, 2 * dist - 1):
                    for sub in range(self.subs):
                        self.copy(z, n, sub, dist).start()

        def passed(self, n):
            block = mod(z - sign(n) * (div(n, 2) + 1) + 2 * NZ, NZ)
            for sub in range(self.subs):
                self.copy(block, n, sub, 1).wait_recv()

                @pl.when((n + 2 < MSGS) & (div(n, 2) + 2 != (self.jump if self.jump > 1 else 0)))
                def _():
                    self.copy(block, n + 2, sub, 1).start()

    acts = Ring(act_all, 1, plan.subs_act, ACT, act_r)
    deltas = Ring(del_all, plan.jump_del, plan.subs_del, DEL, del_r)

    def block_rows(buf, cx, cy, part=None, core=None):
        start = ((cx * Y + cy) * 2 + (c if core is None else core)) * TL
        if part is None:
            return rows(buf, start, TL)
        return rows(buf, start + part * HALF, HALF)

    class Gather:
        def __init__(self, buf, ssem, a_r, b_r, s_r):
            self.buf, self.ssem, self.a_r, self.b_r, self.s_r = buf, ssem, a_r, b_r, s_r

        def copy(self, cx, cy, part, sem, dev, core=None):
            ref = block_rows(self.buf, cx, cy, part, core)
            return remote(ref, ref, self.ssem, sem.at[cx * Y + cy], dev)

        def to_sib(self, cx, cy):
            return self.copy(cx, cy, None, self.s_r, sib)

        def from_sib(self, cx, cy):
            return self.copy(cx, cy, None, self.s_r, sib, 1 - c)

        def first(self):
            for j in PEERS(X):
                self.copy(x, y, None, self.a_r, chip(x_peer(j), y)).start()
            for j in PEERS(Y):
                self.copy(x, y, None, self.a_r, chip(x, y_peer(j))).start()
            self.to_sib(x, y).start()

        def second_a(self, cx):
            self.copy(cx, y, None, self.a_r, sib).wait_recv()
            for k in PEERS(Y):
                self.copy(cx, y, 0, self.a_r, chip(x, y_peer(k))).start()
            self.to_sib(cx, y).start()

        def second_b(self, cy):
            self.copy(x, cy, None, self.a_r, sib).wait_recv()
            for k in PEERS(X):
                self.copy(x, cy, 1, self.b_r, chip(x_peer(k), y)).start()
            self.to_sib(x, cy).start()

        def third(self, cx, cy):
            self.copy(cx, cy, 0, self.a_r, sib).wait_recv()
            self.copy(cx, cy, 1, self.b_r, sib).wait_recv()
            self.to_sib(cx, cy).start()

        def sent(self):
            size = (X + Y - 2) * TL + (X - 1) * (Y - 1) * 2 * HALF + X * Y * TL
            whole = rows(self.buf, 0, size)
            remote(whole, whole, self.ssem, self.s_r.at[0], sib).wait_send()

    THIRDS = (X - 1) * (Y - 1)
    og = Gather(og_all, OG, og_a_r, og_b_r, og_sib_r)
    inp = Gather(in_all, IN, in_a_r, in_b_r, in_sib_r)

    def loop(low, high, body):
        def step(i, _):
            body(i)
            return 0

        lax.fori_loop(low, high, step, 0)

    barrier = pltpu.get_barrier_semaphore()
    friends = [sib]
    for hops in sorted({1, plan.jump_rs, plan.jump_del}):
        friends += [plane(hops), plane(-hops)]
    friends += [chip(x_peer(j), y) for j in range(1, X)]
    friends += [chip(x, y_peer(j)) for j in range(1, Y)]
    for friend in friends:
        pl.semaphore_signal(barrier, inc=1, device_id=friend, device_id_type=MESH)
    get_pre = pltpu.make_async_copy(pre_ref, pre, load.at[0])
    get_og = pltpu.make_async_copy(og_ref, rows(og_all, r * TL, TL), load.at[1])
    get_wout = pltpu.make_async_copy(wout_ref, wout, load.at[2])
    get_in = pltpu.make_async_copy(in_ref, rows(in_all, r * TL, TL), load.at[3])
    get_win = pltpu.make_async_copy(win_ref, win, load.at[4])
    get_adam = [
        pltpu.make_async_copy(ref, buf, load.at[5 + k])
        for k, (ref, buf) in enumerate(
            (
                (moment_out_ref, moments_out),
                (second_out_ref, seconds_out),
                (moment_in_ref, moments_in),
                (second_in_ref, seconds_in),
            )
        )
    ]
    for get in [get_og, get_pre, get_wout, get_in, get_win] + get_adam:
        get.start()
    block = pl.ds(pl.multiple_of(z * TB, 16), TB)
    LONG, SHORT, JUMP = plan.long, plan.short, plan.jump_rs
    FAR, OWN = LONG + 1, LONG + 2
    fresh = [(0, LONG), (1, SHORT), (1, OWN)]
    if JUMP > 1:
        fresh += [(0, JUMP - 1), (1, JUMP - 1)]
    for way, slot in fresh:
        ring[way, slot] = jnp.zeros((TB, plan.FL), BF)
    gin_ref[...] = jnp.zeros_like(gin_ref)
    gout_ref[...] = jnp.zeros_like(gout_ref)
    get_og.wait()
    pl.semaphore_wait(barrier, len(friends))

    late = jnp.minimum(mod(q - z + NZ, NZ), mod(z - q + NZ, NZ)) < plan.early

    @pl.when(jnp.logical_not(late))
    def _():
        og.first()

    get_pre.wait()
    act, slope = gelu_parts(pre[...])
    act_all[block] = act.astype(BF)
    acts.start()

    @pl.when(late)
    def _():
        og.first()

    slopes[...] = slope
    get_in.wait()
    get_wout.wait()
    get_win.wait()

    def needed(n):
        way = mod(n, 2)
        k = div(n, 2) + way
        dist = LONG - k
        if JUMP > 1:
            dist = dist - at_step(k, LONG - JUMP) + at_step(k, LONG - JUMP + 1)
        return way, dist, mod(z + (1 - 2 * way) * sgn * dist + NZ, NZ)

    def og_near(n):
        t = needed(n)[2]
        tx, ty = div(t, Y), mod(t, Y)

        @pl.when((tx != x) & (ty == y))
        def _():
            og.second_a(tx)

        @pl.when((tx == x) & (ty != y))
        def _():
            og.second_b(ty)

    def og_far(n):
        t = needed(n)[2]
        tx, ty = div(t, Y), mod(t, Y)

        @pl.when((tx != x) & (ty != y))
        def _():
            og.third(tx, ty)

    LEAD = plan.lead
    loop(0, NZ, og_near)
    loop(0, plan.act_1, acts.passed)
    loop(0, LEAD, og_far)
    loop(plan.act_1, plan.act_2, acts.passed)

    def rs_copy(way, dist, sub):
        size = TB // plan.subs_rs
        here = pl.ds(sub * size, size)
        direct = at_step(dist, JUMP)
        into = dist - 1 + direct * (FAR - JUMP + 1)
        hops = 1 + direct * (JUMP - 1)
        return remote(
            ring.at[way, dist, here],
            ring.at[way, into, here],
            RS,
            rs_r.at[way, into, sub],
            plane((1 - 2 * way) * sgn * hops),
        )

    def rs_got(way, slot, sub):
        size = TB // plan.subs_rs
        ref = ring.at[way, slot, pl.ds(sub * size, size)]
        return remote(ref, ref, RS, rs_r.at[way, slot, sub], sib)

    def rs_step(n):
        way, dist, t = needed(n)

        @pl.when(n + LEAD < NZ)
        def _():
            og_far(n + LEAD)

        og.from_sib(div(t, Y), mod(t, Y)).wait_recv()
        at = pl.multiple_of(t * TB, 16)
        part = nt_dot(og_all[pl.ds(at, TB)], wout[...]).astype(BF).astype(F32)
        size = TB // plan.subs_rs
        slot = jnp.where(dist == 0, OWN, dist)
        for sub in range(plan.subs_rs):
            here = pl.ds(sub * size, size)

            @pl.when((n >= 2) & (dist != (JUMP - 1 if JUMP > 1 else 0)) & (dist != 0))
            def _():
                rs_got(way, dist, sub).wait_recv()

            ring[way, slot, here] = (
                ring[way, slot, here].astype(F32) + part[sub * size : (sub + 1) * size]
            ).astype(BF)

            @pl.when(dist != 0)
            def _():
                rs_copy(way, dist, sub).start()

        m = plan.act_2 + div(n, plan.act_every)

        @pl.when((mod(n, plan.act_every) == plan.act_every - 1) & (m < plan.act_3))
        def _():
            acts.passed(m)

        @pl.when(n == plan.in_1)
        def _():
            inp.first()

        @pl.when((n > NZ - THIRDS - X) & (n < NZ - THIRDS))
        def _():
            j = n - (NZ - THIRDS - X)
            inp.second_a(x_peer(j))
            inp.second_b(y_peer(j))

        @pl.when((n >= NZ - THIRDS))
        def _():
            i = n - (NZ - THIRDS)
            inp.third(x_peer(div(i, Y - 1) + 1), y_peer(mod(i, Y - 1) + 1))

    loop(0, NZ, rs_step)
    total = ring[1, OWN].astype(F32)
    for slot in (0, FAR) if JUMP > 1 else (FAR,):
        for way in (0, 1):
            for sub in range(plan.subs_rs):
                rs_got(way, slot, sub).wait_recv()
            total = total + ring[way, slot].astype(F32)
    del_all[block] = (total * slopes[...]).astype(BF)
    deltas.start()
    loop(0, X * Y, lambda i: inp.from_sib(div(i, Y), mod(i, Y)).wait_recv())

    def far(i):
        k = div(i + 1, 2)
        return k + at_step(k, 2) - at_step(k, 3) if plan.jump_del == 3 else k

    def message(i):
        return 2 * far(i) - 1 - mod(i, 2)

    def token_block(i, hops):
        sig = (2 * mod(i, 2) - 1) * sgn
        return mod(z - sig * hops + 2 * NZ, NZ)

    def chunk(i):
        return token_block(i, far(i))

    def sib_copy(t):
        return remote(sib_out.at[t], sib_in.at[t], SIB, sib_r.at[t], sib)

    low, high = pl.ds(0, HALF), pl.ds(HALF, HALF)

    def a_copy(t):
        tx, ty = div(t, Y), mod(t, Y)
        return remote(own.at[t, low], rv_a.at[ty, x], RA, ra_r.at[ty, x], chip(tx, y))

    def a_got(ty, sx):
        return remote(rv_a.at[ty, sx], rv_a.at[ty, sx], RA, ra_r.at[ty, sx], sib)

    def b_copy(t):
        tx, ty = div(t, Y), mod(t, Y)
        return remote(own.at[t, high], rv_b.at[tx, y], RB, rb_r.at[tx, y], chip(x, ty))

    def b_got(tx, sy):
        return remote(rv_b.at[tx, sy], rv_b.at[tx, sy], RB, rb_r.at[tx, sy], sib)

    def fa_copy(ty):
        return remote(st_a.at[ty], fin_a.at[y], FA, fa_r.at[y], chip(x, ty))

    def fb_copy(tx):
        return remote(st_b.at[tx], fin_b.at[x], FB, fb_r.at[x], chip(tx, y))

    def arrive(i):
        @pl.when(i >= 1)
        def _():
            deltas.passed(message(i))

        t = chunk(i)
        at = pl.multiple_of(t * TB, 16)
        here = pl.ds(at, TB)
        both = nt_dot(del_all[here], win[...]).astype(BF)
        halves = (both[:TL], both[TL:])
        sib_out[t] = jnp.where(c == 0, halves[1], halves[0])
        sib_copy(t).start()
        own[t] = jnp.where(c == 0, halves[0], halves[1])
        gin_ref[...] += tn_dot(in_all[here], del_all[here])

    def add_out(i):
        here = pl.ds(pl.multiple_of(token_block(i, div(i + 1, 2)) * TB, 16), TB)
        gout_ref[...] += tn_dot(act_all[here], og_all[here])

    def pair(i):
        t = chunk(i)
        sib_copy(t).wait_recv()
        own[t] = (own[t].astype(F32) + sib_in[t].astype(F32)).astype(BF)

        @pl.when(div(t, Y) != x)
        def _():
            a_copy(t).start()

        @pl.when(mod(t, Y) != y)
        def _():
            b_copy(t).start()

    def line(i):
        t = chunk(i)
        tx, ty = div(t, Y), mod(t, Y)

        @pl.when(tx == x)
        def _():
            total = own[t, low].astype(F32)
            for j in range(1, X):
                a_got(ty, x_peer(j)).wait_recv()
                total = total + rv_a[ty, x_peer(j)].astype(F32)
            st_a[ty] = total.astype(BF)

            @pl.when(ty != y)
            def _():
                fa_copy(ty).start()

        @pl.when(ty == y)
        def _():
            total = own[t, high].astype(F32)
            for j in range(1, Y):
                b_got(tx, y_peer(j)).wait_recv()
                total = total + rv_b[tx, y_peer(j)].astype(F32)
            st_b[tx] = total.astype(BF)

            @pl.when(tx != x)
            def _():
                fb_copy(tx).start()

    ROWS = plan.adam_rows

    def adam(weight, moment, second, grads, low, high):
        def some(k):
            here = pl.ds(pl.multiple_of(k * ROWS, ROWS), ROWS)
            new = adam_step(weight[here], moment[here], second[here], grads[here])
            weight[here], moment[here], second[here] = new

        loop(low, high, some)

    put_out = [
        pltpu.make_async_copy(buf, ref, load.at[9 + k])
        for k, (ref, buf) in enumerate(
            ((new_wout_ref, wout), (new_moment_out_ref, moments_out), (new_second_out_ref, seconds_out))
        )
    ]
    put_in = [
        pltpu.make_async_copy(buf, ref, load.at[12 + k])
        for k, (ref, buf) in enumerate(
            ((new_win_ref, win), (new_moment_in_ref, moments_in), (new_second_in_ref, seconds_in))
        )
    ]

    LAG1, LAG2 = plan.lag1, plan.lag2

    def del_step(i):
        arrive(i)

        @pl.when(i <= plan.act_3)
        def _():
            add_out(i)

        @pl.when((i >= plan.act_4) & (i < plan.act_4 + MSGS - plan.act_3))
        def _():
            acts.passed(plan.act_3 + i - plan.act_4)
            add_out(plan.act_3 + i - plan.act_4 + 1)

        @pl.when(i >= LAG1)
        def _():
            pair(i - LAG1)

        @pl.when(i >= LAG2)
        def _():
            line(i - LAG2)

    loop(0, NZ, del_step)
    for get in get_adam:
        get.wait()
    loop(NZ - LAG1, NZ - 1, pair)
    blocks = plan.FL // ROWS
    adam(wout, moments_out, seconds_out, gout_ref, 0, blocks // 2)
    pair(NZ - 1)
    loop(NZ - LAG2, NZ - 1, line)
    adam(wout, moments_out, seconds_out, gout_ref, blocks // 2, blocks)
    for put in put_out:
        put.start()
    blocks = plan.DL // ROWS
    adam(win, moments_in, seconds_in, gin_ref, 0, blocks // 2)
    line(NZ - 1)
    adam(win, moments_in, seconds_in, gin_ref, blocks // 2, blocks)
    for put in put_in:
        put.start()

    og.sent()
    inp.sent()
    messages = rows(act_all, 0, MSGS * TB)
    remote(messages, messages, ACT, act_r.at[0, 0], sib).wait_send()
    remote(messages, messages, DEL, del_r.at[0, 0], sib).wait_send()
    remote(messages, messages, RS, act_r.at[0, 0], sib).wait_send()
    remote(sib_out, sib_out, SIB, sib_r.at[0], sib).wait_send()
    halves = sib_out.at[pl.ds(0, (X - 1) * Y // 2)]
    remote(halves, halves, RA, sib_r.at[0], sib).wait_send()
    halves = sib_out.at[pl.ds(0, (Y - 1) * X // 2)]
    remote(halves, halves, RB, sib_r.at[0], sib).wait_send()

    total = st_a[y].astype(F32)
    for j in range(1, Y):
        remote(fin_a.at[y_peer(j)], fin_a.at[y_peer(j)], FA, fa_r.at[y_peer(j)], sib).wait_recv()
        total = total + fin_a[y_peer(j)].astype(F32)
    ig_ref[low] = total.astype(BF)
    total = st_b[x].astype(F32)
    for j in range(1, X):
        remote(fin_b.at[x_peer(j)], fin_b.at[x_peer(j)], FB, fb_r.at[x_peer(j)], sib).wait_recv()
        total = total + fin_b[x_peer(j)].astype(F32)
    ig_ref[high] = total.astype(BF)
    for put in put_out + put_in:
        put.wait()
    last = st_a.at[pl.ds(0, Y - 1)]
    remote(last, last, FA, fa_r.at[0], sib).wait_send()
    last = st_b.at[pl.ds(0, X - 1)]
    remote(last, last, FB, fb_r.at[0], sib).wait_send()


def exchange(plan, *operands):
    X, Y, NZ, TL, TB, DL, FL = plan.X, plan.Y, plan.nz, plan.TL, plan.TB, plan.DL, plan.FL
    nq, msgs = plan.nq, plan.msgs
    dma = pltpu.SemaphoreType.DMA
    vmem = pl.BlockSpec(memory_space=pltpu.VMEM)
    hbm = pl.BlockSpec(memory_space=pltpu.HBM)
    return pl.pallas_call(
        functools.partial(kernel, plan),
        out_shape=(jax.ShapeDtypeStruct((TL, DL), BF),)
        + (jax.ShapeDtypeStruct((DL, FL), BF),) * 3
        + (jax.ShapeDtypeStruct((FL, DL), BF),) * 3,
        in_specs=[hbm] * 9,
        out_specs=(vmem,) + (hbm,) * 6,
        scratch_shapes=[
            pltpu.VMEM((nq * TB, DL), BF),
            pltpu.VMEM((nq * TB, DL), BF),
            pltpu.VMEM((NZ * TB, FL), BF),
            pltpu.VMEM((NZ * TB, FL), BF),
            pltpu.VMEM((TB, FL), BF),
            pltpu.VMEM((DL, FL), BF),
            pltpu.VMEM((FL, DL), BF),
            pltpu.VMEM((DL, FL), BF),
            pltpu.VMEM((DL, FL), BF),
            pltpu.VMEM((FL, DL), BF),
            pltpu.VMEM((FL, DL), BF),
            pltpu.VMEM((DL, FL), F32),
            pltpu.VMEM((FL, DL), F32),
            pltpu.VMEM((TB, FL), F32),
            pltpu.VMEM((2, plan.long + 3, TB, FL), BF),
            pltpu.VMEM((NZ, TL, DL), BF),
            pltpu.VMEM((NZ, TL, DL), BF),
            pltpu.VMEM((NZ, TL, DL), BF),
            pltpu.VMEM((Y, X, TL // 2, DL), BF),
            pltpu.VMEM((X, Y, TL // 2, DL), BF),
            pltpu.VMEM((Y, TL // 2, DL), BF),
            pltpu.VMEM((X, TL // 2, DL), BF),
            pltpu.VMEM((Y, TL // 2, DL), BF),
            pltpu.VMEM((X, TL // 2, DL), BF),
            dma((15,)),
            dma((10,)),
            dma((msgs, plan.subs_act)),
            dma((2, plan.long + 2, plan.subs_rs)),
            dma((msgs, plan.subs_del)),
        ]
        + [dma((nq,))] * 7
        + [dma((Y, X)), dma((X, Y)), dma((Y,)), dma((X,))],
        compiler_params=pltpu.CompilerParams(
            collective_id=plan.call, has_side_effects=True, vmem_limit_bytes=60 * 1024 * 1024
        ),
    )(*operands)


def hand_over(*refs):
    n = len(refs) // 2
    copies = [pltpu.make_async_copy(refs[k], refs[n + k], refs[-1].at[k]) for k in range(n)]
    for copy in copies:
        copy.start()
    for copy in copies:
        copy.wait()


def results(*arrays):
    hbm = pl.BlockSpec(memory_space=pltpu.HBM)
    return pl.pallas_call(
        hand_over,
        out_shape=tuple(jax.ShapeDtypeStruct(a.shape, a.dtype) for a in arrays),
        in_specs=[hbm] * len(arrays),
        out_specs=(hbm,) * len(arrays),
        scratch_shapes=[pltpu.SemaphoreType.DMA((len(arrays),))],
        compiler_params=pltpu.CompilerParams(vmem_limit_bytes=60 * 1024 * 1024),
    )(*arrays)


def shards(
    plan, inputs, out_grad, preact, weight_in, weight_out, moment_in, second_in, moment_out, second_out
):
    return results(
        *exchange(
            plan,
            out_grad,
            inputs,
            preact,
            weight_in,
            weight_out,
            moment_in,
            second_in,
            moment_out,
            second_out,
        )
    )


def solution(mesh):
    n_row, n_col = mesh.shape["row"], mesh.shape["col"]

    def whole(inputs, out_grad, preact, *rest):
        plan = Plan(
            n_row, n_col, inputs.shape[0] // n_row, inputs.shape[1] // n_col, preact.shape[1] // n_row
        )
        by_token, by_weight = P("row", "col"), P("col", "row")
        return jax.shard_map(
            functools.partial(shards, plan),
            mesh=mesh,
            in_specs=(
                by_token,
                by_token,
                by_weight,
                by_weight,
                by_token,
                by_weight,
                by_weight,
                by_token,
                by_token,
            ),
            out_specs=(by_token, by_weight, by_weight, by_weight, by_token, by_token, by_token),
            check_vma=False,
        )(inputs, out_grad, preact, *rest)

    return whole
```

```python
import functools
import math

import jax
import jax.numpy as jnp
from jax import lax
from jax.experimental import pallas as pl
from jax.experimental.pallas import tpu as pltpu
from jax.sharding import PartitionSpec as P

gelu_coef = 0.7978845608
beta_first = 0.9
beta_second = 0.95
learn_rate = 0.003
epsilon_adam = 1e-08
correct_first = 1.0 - 0.9**10
correct_second = 1.0 - 0.95**10

MESH = pl.DeviceIdType.MESH
BF = jnp.bfloat16
F32 = jnp.float32


def PEERS(n):
    return (1, n - 1) + tuple(range(2, n - 1)) if n > 2 else (1,)


def gelu_parts(preact):
    values = preact.astype(jnp.float32)
    tangent = jnp.tanh(gelu_coef * (values + 0.044715 * values * values * values))
    activated = 0.5 * values * (1.0 + tangent)
    slopes = 0.5 * (1.0 + tangent) + 0.5 * values * (1.0 - tangent * tangent) * gelu_coef * (
        1.0 + 3.0 * 0.044715 * values * values
    )
    return (activated, slopes)


def adam_step(weight, moment, second, grads):
    first_new = beta_first * moment.astype(jnp.float32) + (1.0 - beta_first) * grads
    second_new = beta_second * second.astype(jnp.float32) + (1.0 - beta_second) * grads * grads
    weight_new = weight.astype(jnp.float32) - learn_rate * (first_new / correct_first) / (
        jnp.sqrt(second_new / correct_second) + epsilon_adam
    )
    return (
        weight_new.astype(jnp.bfloat16),
        first_new.astype(jnp.bfloat16),
        second_new.astype(jnp.bfloat16),
    )


def nt_dot(left, right):
    return lax.dot_general(left, right, (((1,), (1,)), ((), ())), preferred_element_type=F32)


def tn_dot(left, right):
    return lax.dot_general(left, right, (((0,), (0,)), ((), ())), preferred_element_type=F32)


class Plan:
    def __init__(self, n_row, n_col, tokens, features, hidden):
        self.nq = n_row // 2
        self.X = math.isqrt(self.nq)
        self.Y = self.nq // self.X
        self.nz = n_col
        self.long = n_col // 2
        self.short = n_col - 1 - self.long
        self.msgs = n_col - 1
        self.TL = tokens
        self.TB = 2 * tokens
        self.DL = features
        self.FL = hidden
        self.subs_act, self.subs_rs, self.subs_del = 2, 4, 4
        self.act_1, self.act_2, self.act_3, self.act_every = 2, 2, 10, 2
        self.lag1, self.lag2 = 3, 7
        self.jump_rs, self.jump_del = 1, 1
        self.lead, self.in_1, self.early, self.act_4 = 4, 2, 5, 11
        self.adam_rows = 32
        self.ops = 2
        self.call = 0


def kernel(
    plan,
    og_ref,
    in_ref,
    pre_ref,
    win_ref,
    wout_ref,
    moment_in_ref,
    second_in_ref,
    moment_out_ref,
    second_out_ref,
    ig_ref,
    new_win_ref,
    new_moment_in_ref,
    new_second_in_ref,
    new_wout_ref,
    new_moment_out_ref,
    new_second_out_ref,
    og_all,
    in_all,
    act_all,
    del_all,
    pre,
    win,
    wout,
    moments_in,
    seconds_in,
    moments_out,
    seconds_out,
    gin_ref,
    gout_ref,
    slopes,
    ring,
    sib_out,
    sib_in,
    own,
    rv_a,
    rv_b,
    st_a,
    st_b,
    fin_a,
    fin_b,
    load,
    sent,
    act_r,
    rs_r,
    del_r,
    og_a_r,
    og_b_r,
    og_sib_r,
    in_a_r,
    in_b_r,
    in_sib_r,
    sib_r,
    ra_r,
    rb_r,
    fa_r,
    fb_r,
):
    X, Y, NZ, TL, TB = plan.X, plan.Y, plan.nz, plan.TL, plan.TB
    HALF, MSGS = TL // 2, plan.msgs
    r = lax.axis_index("row")
    z = lax.axis_index("col")

    def div(a, n):
        if isinstance(a, int):
            return a // n
        if plan.ops == 2 and n & (n - 1) == 0:
            return lax.shift_right_logical(a, jnp.int32(n.bit_length() - 1))
        return lax.div(a, jnp.int32(n)) if plan.ops else a // n

    def mod(a, n):
        if isinstance(a, int):
            return a % n
        if plan.ops == 2 and n & (n - 1) == 0:
            return a & (n - 1)
        return lax.rem(a, jnp.int32(n)) if plan.ops else a % n

    q = div(r, 2)
    c = mod(r, 2)
    x = div(q, Y)
    y = mod(q, Y)
    sgn = 1 - 2 * c
    sib = (r + sgn, z)
    OG, IN, ACT, RS, DEL, SIB, RA, RB, FA, FB = (sent.at[k] for k in range(10))

    def chip(cx, cy):
        return ((cx * Y + cy) * 2 + c, z)

    def x_peer(j):
        return mod(x + j, X)

    def y_peer(j):
        return mod(y + j, Y)

    def remote(src, dst, ssem, rsem, dev):
        return pltpu.make_async_remote_copy(
            src_ref=src, dst_ref=dst, send_sem=ssem, recv_sem=rsem, device_id=dev, device_id_type=MESH
        )

    def rows(buf, start, size):
        return buf.at[pl.ds(pl.multiple_of(start, 16), size)]

    def sign(n):
        return (1 - 2 * mod(n, 2)) * sgn

    def plane(step):
        return (r, mod(z + step + NZ, NZ))

    def at_step(i, a):
        return jnp.where(i == a, 1, 0)

    class Ring:
        def __init__(self, buf, jump, subs, ssem, rsem):
            self.buf, self.jump, self.subs, self.ssem, self.rsem = buf, jump, subs, ssem, rsem

        def copy(self, block, n, sub, hops):
            size = TB // self.subs
            part = rows(self.buf, block * TB + sub * size, size)
            return remote(part, part, self.ssem, self.rsem.at[n, sub], plane(sign(n) * hops))

        def start(self):
            for dist in (1, self.jump) if self.jump > 1 else (1,):
                for n in (2 * dist - 2, 2 * dist - 1):
                    for sub in range(self.subs):
                        self.copy(z, n, sub, dist).start()

        def passed(self, n):
            block = mod(z - sign(n) * (div(n, 2) + 1) + 2 * NZ, NZ)
            for sub in range(self.subs):
                self.copy(block, n, sub, 1).wait_recv()

                @pl.when((n + 2 < MSGS) & (div(n, 2) + 2 != (self.jump if self.jump > 1 else 0)))
                def _():
                    self.copy(block, n + 2, sub, 1).start()

    acts = Ring(act_all, 1, plan.subs_act, ACT, act_r)
    deltas = Ring(del_all, plan.jump_del, plan.subs_del, DEL, del_r)

    def block_rows(buf, cx, cy, part=None, core=None):
        start = ((cx * Y + cy) * 2 + (c if core is None else core)) * TL
        if part is None:
            return rows(buf, start, TL)
        return rows(buf, start + part * HALF, HALF)

    class Gather:
        def __init__(self, source, buf, ssem, a_r, b_r, s_r):
            self.source, self.buf, self.ssem, self.a_r, self.b_r, self.s_r = source, buf, ssem, a_r, b_r, s_r

        def copy(self, cx, cy, part, sem, dev, core=None):
            ref = block_rows(self.buf, cx, cy, part, core)
            return remote(ref, ref, self.ssem, sem.at[cx * Y + cy], dev)

        def to_sib(self, cx, cy):
            return self.copy(cx, cy, None, self.s_r, sib)

        def from_sib(self, cx, cy):
            return self.copy(cx, cy, None, self.s_r, sib, 1 - c)

        def first(self):
            ref = block_rows(self.buf, x, y)
            for j in PEERS(X):
                remote(self.source, ref, self.ssem, self.a_r.at[q], chip(x_peer(j), y)).start()
            for j in PEERS(Y):
                remote(self.source, ref, self.ssem, self.a_r.at[q], chip(x, y_peer(j))).start()
            remote(self.source, ref, self.ssem, self.s_r.at[q], sib).start()

        def second_a(self, cx):
            self.copy(cx, y, None, self.a_r, sib).wait_recv()
            for k in PEERS(Y):
                self.copy(cx, y, 0, self.a_r, chip(x, y_peer(k))).start()
            self.to_sib(cx, y).start()

        def second_b(self, cy):
            self.copy(x, cy, None, self.a_r, sib).wait_recv()
            for k in PEERS(X):
                self.copy(x, cy, 1, self.b_r, chip(x_peer(k), y)).start()
            self.to_sib(x, cy).start()

        def third(self, cx, cy):
            self.copy(cx, cy, 0, self.a_r, sib).wait_recv()
            self.copy(cx, cy, 1, self.b_r, sib).wait_recv()
            self.to_sib(cx, cy).start()

        def sent(self):
            size = (X + Y - 2) * TL + (X - 1) * (Y - 1) * 2 * HALF + X * Y * TL
            whole = rows(self.buf, 0, size)
            remote(whole, whole, self.ssem, self.s_r.at[0], sib).wait_send()

    THIRDS = (X - 1) * (Y - 1)
    og = Gather(og_ref, og_all, OG, og_a_r, og_b_r, og_sib_r)
    inp = Gather(in_ref, in_all, IN, in_a_r, in_b_r, in_sib_r)

    def loop(low, high, body):
        def step(i, _):
            body(i)
            return 0

        lax.fori_loop(low, high, step, 0)

    barrier = pltpu.get_barrier_semaphore()
    friends = [sib]
    for hops in sorted({1, plan.jump_rs, plan.jump_del}):
        friends += [plane(hops), plane(-hops)]
    friends += [chip(x_peer(j), y) for j in range(1, X)]
    friends += [chip(x, y_peer(j)) for j in range(1, Y)]
    for friend in friends:
        pl.semaphore_signal(barrier, inc=1, device_id=friend, device_id_type=MESH)
    get_pre = pltpu.make_async_copy(pre_ref, pre, load.at[0])
    get_og = pltpu.make_async_copy(og_ref, rows(og_all, r * TL, TL), load.at[1])
    get_wout = pltpu.make_async_copy(wout_ref, wout, load.at[2])
    get_in = pltpu.make_async_copy(in_ref, rows(in_all, r * TL, TL), load.at[3])
    get_win = pltpu.make_async_copy(win_ref, win, load.at[4])
    get_adam = [
        pltpu.make_async_copy(ref, buf, load.at[5 + k])
        for k, (ref, buf) in enumerate(
            (
                (moment_out_ref, moments_out),
                (second_out_ref, seconds_out),
                (moment_in_ref, moments_in),
                (second_in_ref, seconds_in),
            )
        )
    ]
    for get in [get_og, get_pre, get_wout, get_in, get_win] + get_adam:
        get.start()
    block = pl.ds(pl.multiple_of(z * TB, 16), TB)
    LONG, SHORT, JUMP = plan.long, plan.short, plan.jump_rs
    FAR, OWN = LONG + 1, LONG + 2
    fresh = [(0, LONG), (1, SHORT), (1, OWN)]
    if JUMP > 1:
        fresh += [(0, JUMP - 1), (1, JUMP - 1)]
    for way, slot in fresh:
        ring[way, slot] = jnp.zeros((TB, plan.FL), BF)
    gin_ref[...] = jnp.zeros_like(gin_ref)
    gout_ref[...] = jnp.zeros_like(gout_ref)
    pl.semaphore_wait(barrier, len(friends))

    late = jnp.minimum(mod(q - z + NZ, NZ), mod(z - q + NZ, NZ)) < plan.early

    @pl.when(jnp.logical_not(late))
    def _():
        og.first()

    get_pre.wait()
    act, slope = gelu_parts(pre[...])
    act_all[block] = act.astype(BF)
    acts.start()

    @pl.when(late)
    def _():
        og.first()

    slopes[...] = slope
    get_og.wait()
    get_in.wait()
    get_wout.wait()
    get_win.wait()

    def needed(n):
        way = mod(n, 2)
        k = div(n, 2) + way
        dist = LONG - k
        if JUMP > 1:
            dist = dist - at_step(k, LONG - JUMP) + at_step(k, LONG - JUMP + 1)
        return way, dist, mod(z + (1 - 2 * way) * sgn * dist + NZ, NZ)

    def og_near(n):
        t = needed(n)[2]
        tx, ty = div(t, Y), mod(t, Y)

        @pl.when((tx != x) & (ty == y))
        def _():
            og.second_a(tx)

        @pl.when((tx == x) & (ty != y))
        def _():
            og.second_b(ty)

    def og_far(n):
        t = needed(n)[2]
        tx, ty = div(t, Y), mod(t, Y)

        @pl.when((tx != x) & (ty != y))
        def _():
            og.third(tx, ty)

    LEAD = plan.lead
    loop(0, NZ, og_near)
    loop(0, plan.act_1, acts.passed)
    loop(0, LEAD, og_far)
    loop(plan.act_1, plan.act_2, acts.passed)

    def rs_copy(way, dist, sub):
        size = TB // plan.subs_rs
        here = pl.ds(sub * size, size)
        direct = at_step(dist, JUMP)
        into = dist - 1 + direct * (FAR - JUMP + 1)
        hops = 1 + direct * (JUMP - 1)
        return remote(
            ring.at[way, dist, here],
            ring.at[way, into, here],
            RS,
            rs_r.at[way, into, sub],
            plane((1 - 2 * way) * sgn * hops),
        )

    def rs_got(way, slot, sub):
        size = TB // plan.subs_rs
        ref = ring.at[way, slot, pl.ds(sub * size, size)]
        return remote(ref, ref, RS, rs_r.at[way, slot, sub], sib)

    def rs_step(n):
        way, dist, t = needed(n)

        @pl.when(n + LEAD < NZ)
        def _():
            og_far(n + LEAD)

        og.from_sib(div(t, Y), mod(t, Y)).wait_recv()
        at = pl.multiple_of(t * TB, 16)
        part = nt_dot(og_all[pl.ds(at, TB)], wout[...]).astype(BF).astype(F32)
        size = TB // plan.subs_rs
        slot = jnp.where(dist == 0, OWN, dist)
        for sub in range(plan.subs_rs):
            here = pl.ds(sub * size, size)

            @pl.when((n >= 2) & (dist != (JUMP - 1 if JUMP > 1 else 0)) & (dist != 0))
            def _():
                rs_got(way, dist, sub).wait_recv()

            ring[way, slot, here] = (
                ring[way, slot, here].astype(F32) + part[sub * size : (sub + 1) * size]
            ).astype(BF)

            @pl.when(dist != 0)
            def _():
                rs_copy(way, dist, sub).start()

        m = plan.act_2 + div(n, plan.act_every)

        @pl.when((mod(n, plan.act_every) == plan.act_every - 1) & (m < plan.act_3))
        def _():
            acts.passed(m)

        @pl.when(n == plan.in_1)
        def _():
            inp.first()

        @pl.when((n > NZ - THIRDS - X) & (n < NZ - THIRDS))
        def _():
            j = n - (NZ - THIRDS - X)
            inp.second_a(x_peer(j))
            inp.second_b(y_peer(j))

        @pl.when((n >= NZ - THIRDS))
        def _():
            i = n - (NZ - THIRDS)
            inp.third(x_peer(div(i, Y - 1) + 1), y_peer(mod(i, Y - 1) + 1))

    loop(0, NZ, rs_step)
    total = ring[1, OWN].astype(F32)
    for slot in (0, FAR) if JUMP > 1 else (FAR,):
        for way in (0, 1):
            for sub in range(plan.subs_rs):
                rs_got(way, slot, sub).wait_recv()
            total = total + ring[way, slot].astype(F32)
    del_all[block] = (total * slopes[...]).astype(BF)
    deltas.start()
    loop(0, X * Y, lambda i: inp.from_sib(div(i, Y), mod(i, Y)).wait_recv())

    def far(i):
        k = div(i + 1, 2)
        return k + at_step(k, 2) - at_step(k, 3) if plan.jump_del == 3 else k

    def message(i):
        return 2 * far(i) - 1 - mod(i, 2)

    def token_block(i, hops):
        sig = (2 * mod(i, 2) - 1) * sgn
        return mod(z - sig * hops + 2 * NZ, NZ)

    def chunk(i):
        return token_block(i, far(i))

    def sib_copy(t):
        return remote(sib_out.at[t], sib_in.at[t], SIB, sib_r.at[t], sib)

    low, high = pl.ds(0, HALF), pl.ds(HALF, HALF)

    def a_copy(t):
        tx, ty = div(t, Y), mod(t, Y)
        return remote(own.at[t, low], rv_a.at[ty, x], RA, ra_r.at[ty, x], chip(tx, y))

    def a_got(ty, sx):
        return remote(rv_a.at[ty, sx], rv_a.at[ty, sx], RA, ra_r.at[ty, sx], sib)

    def b_copy(t):
        tx, ty = div(t, Y), mod(t, Y)
        return remote(own.at[t, high], rv_b.at[tx, y], RB, rb_r.at[tx, y], chip(x, ty))

    def b_got(tx, sy):
        return remote(rv_b.at[tx, sy], rv_b.at[tx, sy], RB, rb_r.at[tx, sy], sib)

    def fa_copy(ty):
        return remote(st_a.at[ty], fin_a.at[y], FA, fa_r.at[y], chip(x, ty))

    def fb_copy(tx):
        return remote(st_b.at[tx], fin_b.at[x], FB, fb_r.at[x], chip(tx, y))

    def arrive(i):
        @pl.when(i >= 1)
        def _():
            deltas.passed(message(i))

        t = chunk(i)
        at = pl.multiple_of(t * TB, 16)
        here = pl.ds(at, TB)
        both = nt_dot(del_all[here], win[...]).astype(BF)
        halves = (both[:TL], both[TL:])
        sib_out[t] = jnp.where(c == 0, halves[1], halves[0])
        sib_copy(t).start()
        own[t] = jnp.where(c == 0, halves[0], halves[1])
        gin_ref[...] += tn_dot(in_all[here], del_all[here])

    def add_out(i):
        here = pl.ds(pl.multiple_of(token_block(i, div(i + 1, 2)) * TB, 16), TB)
        gout_ref[...] += tn_dot(act_all[here], og_all[here])

    def pair(i):
        t = chunk(i)
        sib_copy(t).wait_recv()
        own[t] = (own[t].astype(F32) + sib_in[t].astype(F32)).astype(BF)

        @pl.when(div(t, Y) != x)
        def _():
            a_copy(t).start()

        @pl.when(mod(t, Y) != y)
        def _():
            b_copy(t).start()

    def line(i):
        t = chunk(i)
        tx, ty = div(t, Y), mod(t, Y)

        @pl.when(tx == x)
        def _():
            total = own[t, low].astype(F32)
            for j in range(1, X):
                a_got(ty, x_peer(j)).wait_recv()
                total = total + rv_a[ty, x_peer(j)].astype(F32)
            st_a[ty] = total.astype(BF)

            @pl.when(ty != y)
            def _():
                fa_copy(ty).start()

        @pl.when(ty == y)
        def _():
            total = own[t, high].astype(F32)
            for j in range(1, Y):
                b_got(tx, y_peer(j)).wait_recv()
                total = total + rv_b[tx, y_peer(j)].astype(F32)
            st_b[tx] = total.astype(BF)

            @pl.when(tx != x)
            def _():
                fb_copy(tx).start()

    ROWS = plan.adam_rows

    def adam(weight, moment, second, grads, low, high):
        def some(k):
            here = pl.ds(pl.multiple_of(k * ROWS, ROWS), ROWS)
            new = adam_step(weight[here], moment[here], second[here], grads[here])
            weight[here], moment[here], second[here] = new

        loop(low, high, some)

    put_out = [
        pltpu.make_async_copy(buf, ref, load.at[9 + k])
        for k, (ref, buf) in enumerate(
            ((new_wout_ref, wout), (new_moment_out_ref, moments_out), (new_second_out_ref, seconds_out))
        )
    ]
    put_in = [
        pltpu.make_async_copy(buf, ref, load.at[12 + k])
        for k, (ref, buf) in enumerate(
            ((new_win_ref, win), (new_moment_in_ref, moments_in), (new_second_in_ref, seconds_in))
        )
    ]

    LAG1, LAG2 = plan.lag1, plan.lag2

    def del_step(i):
        arrive(i)

        @pl.when(i <= plan.act_3)
        def _():
            add_out(i)

        @pl.when((i >= plan.act_4) & (i < plan.act_4 + MSGS - plan.act_3))
        def _():
            acts.passed(plan.act_3 + i - plan.act_4)
            add_out(plan.act_3 + i - plan.act_4 + 1)

        @pl.when(i >= LAG1)
        def _():
            pair(i - LAG1)

        @pl.when(i >= LAG2)
        def _():
            line(i - LAG2)

    loop(0, NZ, del_step)
    for get in get_adam:
        get.wait()
    loop(NZ - LAG1, NZ - 1, pair)
    blocks = plan.FL // ROWS
    adam(wout, moments_out, seconds_out, gout_ref, 0, blocks // 2)
    pair(NZ - 1)
    loop(NZ - LAG2, NZ - 1, line)
    adam(wout, moments_out, seconds_out, gout_ref, blocks // 2, blocks)
    for put in put_out:
        put.start()
    blocks = plan.DL // ROWS
    adam(win, moments_in, seconds_in, gin_ref, 0, blocks // 2)
    line(NZ - 1)
    adam(win, moments_in, seconds_in, gin_ref, blocks // 2, blocks)
    for put in put_in:
        put.start()

    og.sent()
    inp.sent()
    messages = rows(act_all, 0, MSGS * TB)
    remote(messages, messages, ACT, act_r.at[0, 0], sib).wait_send()
    remote(messages, messages, DEL, del_r.at[0, 0], sib).wait_send()
    remote(messages, messages, RS, act_r.at[0, 0], sib).wait_send()
    remote(sib_out, sib_out, SIB, sib_r.at[0], sib).wait_send()
    halves = sib_out.at[pl.ds(0, (X - 1) * Y // 2)]
    remote(halves, halves, RA, sib_r.at[0], sib).wait_send()
    halves = sib_out.at[pl.ds(0, (Y - 1) * X // 2)]
    remote(halves, halves, RB, sib_r.at[0], sib).wait_send()

    total = st_a[y].astype(F32)
    for j in range(1, Y):
        remote(fin_a.at[y_peer(j)], fin_a.at[y_peer(j)], FA, fa_r.at[y_peer(j)], sib).wait_recv()
        total = total + fin_a[y_peer(j)].astype(F32)
    ig_ref[low] = total.astype(BF)
    total = st_b[x].astype(F32)
    for j in range(1, X):
        remote(fin_b.at[x_peer(j)], fin_b.at[x_peer(j)], FB, fb_r.at[x_peer(j)], sib).wait_recv()
        total = total + fin_b[x_peer(j)].astype(F32)
    ig_ref[high] = total.astype(BF)
    for put in put_out + put_in:
        put.wait()
    last = st_a.at[pl.ds(0, Y - 1)]
    remote(last, last, FA, fa_r.at[0], sib).wait_send()
    last = st_b.at[pl.ds(0, X - 1)]
    remote(last, last, FB, fb_r.at[0], sib).wait_send()


def exchange(plan, *operands):
    X, Y, NZ, TL, TB, DL, FL = plan.X, plan.Y, plan.nz, plan.TL, plan.TB, plan.DL, plan.FL
    nq, msgs = plan.nq, plan.msgs
    dma = pltpu.SemaphoreType.DMA
    vmem = pl.BlockSpec(memory_space=pltpu.VMEM)
    hbm = pl.BlockSpec(memory_space=pltpu.HBM)
    return pl.pallas_call(
        functools.partial(kernel, plan),
        out_shape=(jax.ShapeDtypeStruct((TL, DL), BF),)
        + (jax.ShapeDtypeStruct((DL, FL), BF),) * 3
        + (jax.ShapeDtypeStruct((FL, DL), BF),) * 3,
        in_specs=[hbm] * 9,
        out_specs=(vmem,) + (hbm,) * 6,
        scratch_shapes=[
            pltpu.VMEM((nq * TB, DL), BF),
            pltpu.VMEM((nq * TB, DL), BF),
            pltpu.VMEM((NZ * TB, FL), BF),
            pltpu.VMEM((NZ * TB, FL), BF),
            pltpu.VMEM((TB, FL), BF),
            pltpu.VMEM((DL, FL), BF),
            pltpu.VMEM((FL, DL), BF),
            pltpu.VMEM((DL, FL), BF),
            pltpu.VMEM((DL, FL), BF),
            pltpu.VMEM((FL, DL), BF),
            pltpu.VMEM((FL, DL), BF),
            pltpu.VMEM((DL, FL), F32),
            pltpu.VMEM((FL, DL), F32),
            pltpu.VMEM((TB, FL), F32),
            pltpu.VMEM((2, plan.long + 3, TB, FL), BF),
            pltpu.VMEM((NZ, TL, DL), BF),
            pltpu.VMEM((NZ, TL, DL), BF),
            pltpu.VMEM((NZ, TL, DL), BF),
            pltpu.VMEM((Y, X, TL // 2, DL), BF),
            pltpu.VMEM((X, Y, TL // 2, DL), BF),
            pltpu.VMEM((Y, TL // 2, DL), BF),
            pltpu.VMEM((X, TL // 2, DL), BF),
            pltpu.VMEM((Y, TL // 2, DL), BF),
            pltpu.VMEM((X, TL // 2, DL), BF),
            dma((15,)),
            dma((10,)),
            dma((msgs, plan.subs_act)),
            dma((2, plan.long + 2, plan.subs_rs)),
            dma((msgs, plan.subs_del)),
        ]
        + [dma((nq,))] * 7
        + [dma((Y, X)), dma((X, Y)), dma((Y,)), dma((X,))],
        compiler_params=pltpu.CompilerParams(
            collective_id=plan.call, has_side_effects=True, vmem_limit_bytes=60 * 1024 * 1024
        ),
    )(*operands)


def hand_over(*refs):
    n = (len(refs) - 2) // 3
    sources, targets, held, (came, left) = refs[:n], refs[n : 2 * n], refs[2 * n : 3 * n], refs[3 * n :]
    loads = [pltpu.make_async_copy(sources[k], held[k], came.at[k]) for k in range(n)]
    stores = [pltpu.make_async_copy(held[k], targets[k], left.at[k]) for k in range(n)]
    for load in loads:
        load.start()
    for load, store in zip(loads, stores):
        load.wait()
        store.start()
    for store in stores:
        store.wait()


def results(*arrays):
    hbm = pl.BlockSpec(memory_space=pltpu.HBM)
    n = len(arrays)
    return pl.pallas_call(
        hand_over,
        out_shape=tuple(jax.ShapeDtypeStruct(a.shape, a.dtype) for a in arrays),
        in_specs=[hbm] * n,
        out_specs=(hbm,) * n,
        scratch_shapes=[pltpu.VMEM(a.shape, a.dtype) for a in arrays] + [pltpu.SemaphoreType.DMA((n,))] * 2,
        compiler_params=pltpu.CompilerParams(vmem_limit_bytes=60 * 1024 * 1024),
    )(*arrays)


def shards(
    plan, inputs, out_grad, preact, weight_in, weight_out, moment_in, second_in, moment_out, second_out
):
    return results(
        *exchange(
            plan,
            out_grad,
            inputs,
            preact,
            weight_in,
            weight_out,
            moment_in,
            second_in,
            moment_out,
            second_out,
        )
    )


def solution(mesh):
    n_row, n_col = mesh.shape["row"], mesh.shape["col"]

    def whole(inputs, out_grad, preact, *rest):
        plan = Plan(
            n_row, n_col, inputs.shape[0] // n_row, inputs.shape[1] // n_col, preact.shape[1] // n_row
        )
        by_token, by_weight = P("row", "col"), P("col", "row")
        return jax.shard_map(
            functools.partial(shards, plan),
            mesh=mesh,
            in_specs=(
                by_token,
                by_token,
                by_weight,
                by_weight,
                by_token,
                by_weight,
                by_weight,
                by_token,
                by_token,
            ),
            out_specs=(by_token, by_weight, by_weight, by_weight, by_token, by_token, by_token),
            check_vma=False,
        )(inputs, out_grad, preact, *rest)

    return whole
```

```python
import functools
import math

import jax
import jax.numpy as jnp
from jax import lax
from jax.experimental import pallas as pl
from jax.experimental.pallas import tpu as pltpu
from jax.sharding import PartitionSpec as P

gelu_coef = 0.7978845608
beta_first = 0.9
beta_second = 0.95
learn_rate = 0.003
epsilon_adam = 1e-08
correct_first = 1.0 - 0.9**10
correct_second = 1.0 - 0.95**10

MESH = pl.DeviceIdType.MESH
BF = jnp.bfloat16
F32 = jnp.float32


def PEERS(n):
    return (1, n - 1) + tuple(range(2, n - 1)) if n > 2 else (1,)


def gelu_parts(preact):
    values = preact.astype(jnp.float32)
    tangent = jnp.tanh(gelu_coef * (values + 0.044715 * values * values * values))
    activated = 0.5 * values * (1.0 + tangent)
    slopes = 0.5 * (1.0 + tangent) + 0.5 * values * (1.0 - tangent * tangent) * gelu_coef * (
        1.0 + 3.0 * 0.044715 * values * values
    )
    return (activated, slopes)


def adam_step(weight, moment, second, grads):
    first_new = beta_first * moment.astype(jnp.float32) + (1.0 - beta_first) * grads
    second_new = beta_second * second.astype(jnp.float32) + (1.0 - beta_second) * grads * grads
    weight_new = weight.astype(jnp.float32) - learn_rate * (first_new / correct_first) / (
        jnp.sqrt(second_new / correct_second) + epsilon_adam
    )
    return (
        weight_new.astype(jnp.bfloat16),
        first_new.astype(jnp.bfloat16),
        second_new.astype(jnp.bfloat16),
    )


def nt_dot(left, right):
    return lax.dot_general(left, right, (((1,), (1,)), ((), ())), preferred_element_type=F32)


def tn_dot(left, right):
    return lax.dot_general(left, right, (((0,), (0,)), ((), ())), preferred_element_type=F32)


class Plan:
    def __init__(self, n_row, n_col, tokens, features, hidden):
        self.nq = n_row // 2
        self.X = math.isqrt(self.nq)
        self.Y = self.nq // self.X
        self.nz = n_col
        self.long = n_col // 2
        self.short = n_col - 1 - self.long
        self.msgs = n_col - 1
        self.TL = tokens
        self.TB = 2 * tokens
        self.DL = features
        self.FL = hidden
        self.subs_act, self.subs_rs, self.subs_del = 2, 4, 4
        self.act_1, self.act_2, self.act_3, self.act_every = 2, 2, 10, 2
        self.lag1, self.lag2 = 3, 6
        self.jump_rs, self.jump_del = 1, 1
        self.lead, self.in_1, self.early, self.act_4 = 1, 2, 5, 11
        self.adam_rows = 32
        self.ops = 2
        self.call = 0


def kernel(
    plan,
    og_ref,
    in_ref,
    pre_ref,
    win_ref,
    wout_ref,
    moment_in_ref,
    second_in_ref,
    moment_out_ref,
    second_out_ref,
    ig_ref,
    new_win_ref,
    new_moment_in_ref,
    new_second_in_ref,
    new_wout_ref,
    new_moment_out_ref,
    new_second_out_ref,
    og_all,
    in_all,
    act_all,
    del_all,
    pre,
    win,
    wout,
    moments_in,
    seconds_in,
    moments_out,
    seconds_out,
    gin_ref,
    gout_ref,
    slopes,
    ring,
    sib_out,
    sib_in,
    own,
    rv_a,
    rv_b,
    st_a,
    st_b,
    fin_a,
    fin_b,
    load,
    sent,
    act_r,
    rs_r,
    del_r,
    og_a_r,
    og_b_r,
    og_sib_r,
    in_a_r,
    in_b_r,
    in_sib_r,
    sib_r,
    ra_r,
    rb_r,
    fa_r,
    fb_r,
):
    X, Y, NZ, TL, TB = plan.X, plan.Y, plan.nz, plan.TL, plan.TB
    HALF, MSGS = TL // 2, plan.msgs
    r = lax.axis_index("row")
    z = lax.axis_index("col")

    def div(a, n):
        if isinstance(a, int):
            return a // n
        if plan.ops == 2 and n & (n - 1) == 0:
            return lax.shift_right_logical(a, jnp.int32(n.bit_length() - 1))
        return lax.div(a, jnp.int32(n)) if plan.ops else a // n

    def mod(a, n):
        if isinstance(a, int):
            return a % n
        if plan.ops == 2 and n & (n - 1) == 0:
            return a & (n - 1)
        return lax.rem(a, jnp.int32(n)) if plan.ops else a % n

    q = div(r, 2)
    c = mod(r, 2)
    x = div(q, Y)
    y = mod(q, Y)
    sgn = 1 - 2 * c
    sib = (r + sgn, z)
    OG, IN, ACT, RS, DEL, SIB, RA, RB, FA, FB = (sent.at[k] for k in range(10))

    def chip(cx, cy):
        return ((cx * Y + cy) * 2 + c, z)

    def x_peer(j):
        return mod(x + j, X)

    def y_peer(j):
        return mod(y + j, Y)

    def remote(src, dst, ssem, rsem, dev):
        return pltpu.make_async_remote_copy(
            src_ref=src, dst_ref=dst, send_sem=ssem, recv_sem=rsem, device_id=dev, device_id_type=MESH
        )

    def rows(buf, start, size):
        return buf.at[pl.ds(pl.multiple_of(start, 16), size)]

    def sign(n):
        return (1 - 2 * mod(n, 2)) * sgn

    def plane(step):
        return (r, mod(z + step + NZ, NZ))

    def at_step(i, a):
        return jnp.where(i == a, 1, 0)

    class Ring:
        def __init__(self, buf, jump, subs, ssem, rsem):
            self.buf, self.jump, self.subs, self.ssem, self.rsem = buf, jump, subs, ssem, rsem

        def copy(self, block, n, sub, hops):
            size = TB // self.subs
            part = rows(self.buf, block * TB + sub * size, size)
            return remote(part, part, self.ssem, self.rsem.at[n, sub], plane(sign(n) * hops))

        def start(self):
            for dist in (1, self.jump) if self.jump > 1 else (1,):
                for n in (2 * dist - 2, 2 * dist - 1):
                    for sub in range(self.subs):
                        self.copy(z, n, sub, dist).start()

        def passed(self, n):
            block = mod(z - sign(n) * (div(n, 2) + 1) + 2 * NZ, NZ)
            for sub in range(self.subs):
                self.copy(block, n, sub, 1).wait_recv()

                @pl.when((n + 2 < MSGS) & (div(n, 2) + 2 != (self.jump if self.jump > 1 else 0)))
                def _():
                    self.copy(block, n + 2, sub, 1).start()

    acts = Ring(act_all, 1, plan.subs_act, ACT, act_r)
    deltas = Ring(del_all, plan.jump_del, plan.subs_del, DEL, del_r)

    def block_rows(buf, cx, cy, part=None, core=None):
        start = ((cx * Y + cy) * 2 + (c if core is None else core)) * TL
        if part is None:
            return rows(buf, start, TL)
        return rows(buf, start + part * HALF, HALF)

    class Gather:
        def __init__(self, source, buf, ssem, a_r, b_r, s_r):
            self.source, self.buf, self.ssem, self.a_r, self.b_r, self.s_r = source, buf, ssem, a_r, b_r, s_r

        def copy(self, cx, cy, part, sem, dev, core=None):
            ref = block_rows(self.buf, cx, cy, part, core)
            return remote(ref, ref, self.ssem, sem.at[cx * Y + cy], dev)

        def to_sib(self, cx, cy):
            return self.copy(cx, cy, None, self.s_r, sib)

        def from_sib(self, cx, cy):
            return self.copy(cx, cy, None, self.s_r, sib, 1 - c)

        def first(self):
            ref = block_rows(self.buf, x, y)
            for j in PEERS(X):
                remote(self.source, ref, self.ssem, self.a_r.at[q], chip(x_peer(j), y)).start()
            for j in PEERS(Y):
                remote(self.source, ref, self.ssem, self.a_r.at[q], chip(x, y_peer(j))).start()
            remote(self.source, ref, self.ssem, self.s_r.at[q], sib).start()

        def second_a(self, cx):
            self.copy(cx, y, None, self.a_r, sib).wait_recv()
            for k in PEERS(Y):
                self.copy(cx, y, 0, self.a_r, chip(x, y_peer(k))).start()
            self.to_sib(cx, y).start()

        def second_b(self, cy):
            self.copy(x, cy, None, self.a_r, sib).wait_recv()
            for k in PEERS(X):
                self.copy(x, cy, 1, self.b_r, chip(x_peer(k), y)).start()
            self.to_sib(x, cy).start()

        def third(self, cx, cy):
            self.copy(cx, cy, 0, self.a_r, sib).wait_recv()
            self.copy(cx, cy, 1, self.b_r, sib).wait_recv()
            self.to_sib(cx, cy).start()

        def sent(self):
            size = (X + Y - 2) * TL + (X - 1) * (Y - 1) * 2 * HALF + X * Y * TL
            whole = rows(self.buf, 0, size)
            remote(whole, whole, self.ssem, self.s_r.at[0], sib).wait_send()

    THIRDS = (X - 1) * (Y - 1)
    og = Gather(og_ref, og_all, OG, og_a_r, og_b_r, og_sib_r)
    inp = Gather(in_ref, in_all, IN, in_a_r, in_b_r, in_sib_r)

    def loop(low, high, body):
        def step(i, _):
            body(i)
            return 0

        lax.fori_loop(low, high, step, 0)

    barrier = pltpu.get_barrier_semaphore()
    friends = [sib]
    for hops in sorted({1, plan.jump_rs, plan.jump_del}):
        friends += [plane(hops), plane(-hops)]
    friends += [chip(x_peer(j), y) for j in range(1, X)]
    friends += [chip(x, y_peer(j)) for j in range(1, Y)]
    for friend in friends:
        pl.semaphore_signal(barrier, inc=1, device_id=friend, device_id_type=MESH)
    get_pre = pltpu.make_async_copy(pre_ref, pre, load.at[0])
    get_og = pltpu.make_async_copy(og_ref, rows(og_all, r * TL, TL), load.at[1])
    get_wout = pltpu.make_async_copy(wout_ref, wout, load.at[2])
    get_in = pltpu.make_async_copy(in_ref, rows(in_all, r * TL, TL), load.at[3])
    get_win = pltpu.make_async_copy(win_ref, win, load.at[4])
    get_adam = [
        pltpu.make_async_copy(ref, buf, load.at[5 + k])
        for k, (ref, buf) in enumerate(
            (
                (moment_out_ref, moments_out),
                (second_out_ref, seconds_out),
                (moment_in_ref, moments_in),
                (second_in_ref, seconds_in),
            )
        )
    ]
    for get in [get_og, get_pre, get_wout, get_in, get_win] + get_adam:
        get.start()
    block = pl.ds(pl.multiple_of(z * TB, 16), TB)
    LONG, SHORT, JUMP = plan.long, plan.short, plan.jump_rs
    FAR, OWN = LONG + 1, LONG + 2
    fresh = [(0, LONG), (1, SHORT), (1, OWN)]
    if JUMP > 1:
        fresh += [(0, JUMP - 1), (1, JUMP - 1)]
    for way, slot in fresh:
        ring[way, slot] = jnp.zeros((TB, plan.FL), BF)
    gin_ref[...] = jnp.zeros_like(gin_ref)
    gout_ref[...] = jnp.zeros_like(gout_ref)
    pl.semaphore_wait(barrier, len(friends))

    late = jnp.minimum(mod(q - z + NZ, NZ), mod(z - q + NZ, NZ)) < plan.early

    @pl.when(jnp.logical_not(late))
    def _():
        og.first()

    get_pre.wait()
    act, slope = gelu_parts(pre[...])
    act_all[block] = act.astype(BF)
    acts.start()

    @pl.when(late)
    def _():
        og.first()

    slopes[...] = slope
    get_og.wait()
    get_in.wait()
    get_wout.wait()
    get_win.wait()

    def needed(n):
        way = mod(n, 2)
        k = div(n, 2) + way
        dist = LONG - k
        if JUMP > 1:
            dist = dist - at_step(k, LONG - JUMP) + at_step(k, LONG - JUMP + 1)
        return way, dist, mod(z + (1 - 2 * way) * sgn * dist + NZ, NZ)

    def og_near(n):
        t = needed(n)[2]
        tx, ty = div(t, Y), mod(t, Y)

        @pl.when((tx != x) & (ty == y))
        def _():
            og.second_a(tx)

        @pl.when((tx == x) & (ty != y))
        def _():
            og.second_b(ty)

    def og_far(n):
        t = needed(n)[2]
        tx, ty = div(t, Y), mod(t, Y)

        @pl.when((tx != x) & (ty != y))
        def _():
            og.third(tx, ty)

    LEAD = plan.lead
    loop(0, NZ, og_near)
    loop(0, plan.act_1, acts.passed)
    loop(0, LEAD, og_far)
    loop(plan.act_1, plan.act_2, acts.passed)

    def rs_copy(way, dist, sub):
        size = TB // plan.subs_rs
        here = pl.ds(sub * size, size)
        direct = at_step(dist, JUMP)
        into = dist - 1 + direct * (FAR - JUMP + 1)
        hops = 1 + direct * (JUMP - 1)
        return remote(
            ring.at[way, dist, here],
            ring.at[way, into, here],
            RS,
            rs_r.at[way, into, sub],
            plane((1 - 2 * way) * sgn * hops),
        )

    def rs_got(way, slot, sub):
        size = TB // plan.subs_rs
        ref = ring.at[way, slot, pl.ds(sub * size, size)]
        return remote(ref, ref, RS, rs_r.at[way, slot, sub], sib)

    def rs_step(n):
        way, dist, t = needed(n)

        @pl.when(n + LEAD < NZ)
        def _():
            og_far(n + LEAD)

        og.from_sib(div(t, Y), mod(t, Y)).wait_recv()
        at = pl.multiple_of(t * TB, 16)
        part = nt_dot(og_all[pl.ds(at, TB)], wout[...]).astype(BF).astype(F32)
        size = TB // plan.subs_rs
        slot = jnp.where(dist == 0, OWN, dist)
        for sub in range(plan.subs_rs):
            here = pl.ds(sub * size, size)

            @pl.when((n >= 2) & (dist != (JUMP - 1 if JUMP > 1 else 0)) & (dist != 0))
            def _():
                rs_got(way, dist, sub).wait_recv()

            ring[way, slot, here] = (
                ring[way, slot, here].astype(F32) + part[sub * size : (sub + 1) * size]
            ).astype(BF)

            @pl.when(dist != 0)
            def _():
                rs_copy(way, dist, sub).start()

        m = plan.act_2 + div(n, plan.act_every)

        @pl.when((mod(n, plan.act_every) == plan.act_every - 1) & (m < plan.act_3))
        def _():
            acts.passed(m)

        @pl.when(n == plan.in_1)
        def _():
            inp.first()

        @pl.when((n > NZ - THIRDS - X) & (n < NZ - THIRDS))
        def _():
            j = n - (NZ - THIRDS - X)
            inp.second_a(x_peer(j))
            inp.second_b(y_peer(j))

        @pl.when((n >= NZ - THIRDS))
        def _():
            i = n - (NZ - THIRDS)
            inp.third(x_peer(div(i, Y - 1) + 1), y_peer(mod(i, Y - 1) + 1))

    loop(0, NZ, rs_step)
    total = ring[1, OWN].astype(F32)
    for slot in (0, FAR) if JUMP > 1 else (FAR,):
        for way in (0, 1):
            for sub in range(plan.subs_rs):
                rs_got(way, slot, sub).wait_recv()
            total = total + ring[way, slot].astype(F32)
    del_all[block] = (total * slopes[...]).astype(BF)
    deltas.start()
    loop(0, X * Y, lambda i: inp.from_sib(div(i, Y), mod(i, Y)).wait_recv())

    def far(i):
        k = div(i + 1, 2)
        return k + at_step(k, 2) - at_step(k, 3) if plan.jump_del == 3 else k

    def message(i):
        return 2 * far(i) - 1 - mod(i, 2)

    def token_block(i, hops):
        sig = (2 * mod(i, 2) - 1) * sgn
        return mod(z - sig * hops + 2 * NZ, NZ)

    def chunk(i):
        return token_block(i, far(i))

    def sib_copy(t):
        return remote(sib_out.at[t], sib_in.at[t], SIB, sib_r.at[t], sib)

    low, high = pl.ds(0, HALF), pl.ds(HALF, HALF)

    def a_copy(t):
        tx, ty = div(t, Y), mod(t, Y)
        return remote(own.at[t, low], rv_a.at[ty, x], RA, ra_r.at[ty, x], chip(tx, y))

    def a_got(ty, sx):
        return remote(rv_a.at[ty, sx], rv_a.at[ty, sx], RA, ra_r.at[ty, sx], sib)

    def b_copy(t):
        tx, ty = div(t, Y), mod(t, Y)
        return remote(own.at[t, high], rv_b.at[tx, y], RB, rb_r.at[tx, y], chip(x, ty))

    def b_got(tx, sy):
        return remote(rv_b.at[tx, sy], rv_b.at[tx, sy], RB, rb_r.at[tx, sy], sib)

    def fa_copy(ty):
        return remote(st_a.at[ty], fin_a.at[y], FA, fa_r.at[y], chip(x, ty))

    def fb_copy(tx):
        return remote(st_b.at[tx], fin_b.at[x], FB, fb_r.at[x], chip(tx, y))

    def arrive(i):
        @pl.when(i >= 1)
        def _():
            deltas.passed(message(i))

        t = chunk(i)
        at = pl.multiple_of(t * TB, 16)
        here = pl.ds(at, TB)
        both = nt_dot(del_all[here], win[...]).astype(BF)
        halves = (both[:TL], both[TL:])
        sib_out[t] = jnp.where(c == 0, halves[1], halves[0])
        sib_copy(t).start()
        own[t] = jnp.where(c == 0, halves[0], halves[1])
        gin_ref[...] += tn_dot(in_all[here], del_all[here])

    def add_out(i):
        here = pl.ds(pl.multiple_of(token_block(i, div(i + 1, 2)) * TB, 16), TB)
        gout_ref[...] += tn_dot(act_all[here], og_all[here])

    def pair(i):
        t = chunk(i)
        sib_copy(t).wait_recv()
        own[t] = (own[t].astype(F32) + sib_in[t].astype(F32)).astype(BF)

        @pl.when(div(t, Y) != x)
        def _():
            a_copy(t).start()

        @pl.when(mod(t, Y) != y)
        def _():
            b_copy(t).start()

    def line(i):
        t = chunk(i)
        tx, ty = div(t, Y), mod(t, Y)

        @pl.when(tx == x)
        def _():
            total = own[t, low].astype(F32)
            for j in range(1, X):
                a_got(ty, x_peer(j)).wait_recv()
                total = total + rv_a[ty, x_peer(j)].astype(F32)
            st_a[ty] = total.astype(BF)

            @pl.when(ty != y)
            def _():
                fa_copy(ty).start()

        @pl.when(ty == y)
        def _():
            total = own[t, high].astype(F32)
            for j in range(1, Y):
                b_got(tx, y_peer(j)).wait_recv()
                total = total + rv_b[tx, y_peer(j)].astype(F32)
            st_b[tx] = total.astype(BF)

            @pl.when(tx != x)
            def _():
                fb_copy(tx).start()

    ROWS = plan.adam_rows

    def adam(weight, moment, second, grads, low, high):
        def some(k):
            here = pl.ds(pl.multiple_of(k * ROWS, ROWS), ROWS)
            new = adam_step(weight[here], moment[here], second[here], grads[here])
            weight[here], moment[here], second[here] = new

        loop(low, high, some)

    put_out = [
        pltpu.make_async_copy(buf, ref, load.at[9 + k])
        for k, (ref, buf) in enumerate(
            ((new_wout_ref, wout), (new_moment_out_ref, moments_out), (new_second_out_ref, seconds_out))
        )
    ]
    put_in = [
        pltpu.make_async_copy(buf, ref, load.at[12 + k])
        for k, (ref, buf) in enumerate(
            ((new_win_ref, win), (new_moment_in_ref, moments_in), (new_second_in_ref, seconds_in))
        )
    ]

    LAG1, LAG2 = plan.lag1, plan.lag2

    def del_step(i):
        arrive(i)

        @pl.when(i <= plan.act_3)
        def _():
            add_out(i)

        @pl.when((i >= plan.act_4) & (i < plan.act_4 + MSGS - plan.act_3))
        def _():
            acts.passed(plan.act_3 + i - plan.act_4)
            add_out(plan.act_3 + i - plan.act_4 + 1)

        @pl.when(i >= LAG1)
        def _():
            pair(i - LAG1)

        @pl.when(i >= LAG2)
        def _():
            line(i - LAG2)

    loop(0, NZ, del_step)
    for get in get_adam:
        get.wait()
    loop(NZ - LAG1, NZ, pair)
    loop(NZ - LAG2, NZ - 1, line)
    adam(wout, moments_out, seconds_out, gout_ref, 0, plan.FL // ROWS)
    for put in put_out:
        put.start()
    blocks = plan.DL // ROWS
    adam(win, moments_in, seconds_in, gin_ref, 0, blocks // 4)
    line(NZ - 1)
    adam(win, moments_in, seconds_in, gin_ref, blocks // 4, blocks)
    for put in put_in:
        put.start()

    og.sent()
    inp.sent()
    messages = rows(act_all, 0, MSGS * TB)
    remote(messages, messages, ACT, act_r.at[0, 0], sib).wait_send()
    remote(messages, messages, DEL, del_r.at[0, 0], sib).wait_send()
    remote(messages, messages, RS, act_r.at[0, 0], sib).wait_send()
    remote(sib_out, sib_out, SIB, sib_r.at[0], sib).wait_send()
    halves = sib_out.at[pl.ds(0, (X - 1) * Y // 2)]
    remote(halves, halves, RA, sib_r.at[0], sib).wait_send()
    halves = sib_out.at[pl.ds(0, (Y - 1) * X // 2)]
    remote(halves, halves, RB, sib_r.at[0], sib).wait_send()

    total = st_a[y].astype(F32)
    for j in range(1, Y):
        remote(fin_a.at[y_peer(j)], fin_a.at[y_peer(j)], FA, fa_r.at[y_peer(j)], sib).wait_recv()
        total = total + fin_a[y_peer(j)].astype(F32)
    ig_ref[low] = total.astype(BF)
    total = st_b[x].astype(F32)
    for j in range(1, X):
        remote(fin_b.at[x_peer(j)], fin_b.at[x_peer(j)], FB, fb_r.at[x_peer(j)], sib).wait_recv()
        total = total + fin_b[x_peer(j)].astype(F32)
    ig_ref[high] = total.astype(BF)
    for put in put_out + put_in:
        put.wait()
    last = st_a.at[pl.ds(0, Y - 1)]
    remote(last, last, FA, fa_r.at[0], sib).wait_send()
    last = st_b.at[pl.ds(0, X - 1)]
    remote(last, last, FB, fb_r.at[0], sib).wait_send()


def exchange(plan, *operands):
    X, Y, NZ, TL, TB, DL, FL = plan.X, plan.Y, plan.nz, plan.TL, plan.TB, plan.DL, plan.FL
    nq, msgs = plan.nq, plan.msgs
    dma = pltpu.SemaphoreType.DMA
    vmem = pl.BlockSpec(memory_space=pltpu.VMEM)
    hbm = pl.BlockSpec(memory_space=pltpu.HBM)
    return pl.pallas_call(
        functools.partial(kernel, plan),
        out_shape=(jax.ShapeDtypeStruct((TL, DL), BF),)
        + (jax.ShapeDtypeStruct((DL, FL), BF),) * 3
        + (jax.ShapeDtypeStruct((FL, DL), BF),) * 3,
        in_specs=[hbm] * 9,
        out_specs=(vmem,) + (hbm,) * 6,
        scratch_shapes=[
            pltpu.VMEM((nq * TB, DL), BF),
            pltpu.VMEM((nq * TB, DL), BF),
            pltpu.VMEM((NZ * TB, FL), BF),
            pltpu.VMEM((NZ * TB, FL), BF),
            pltpu.VMEM((TB, FL), BF),
            pltpu.VMEM((DL, FL), BF),
            pltpu.VMEM((FL, DL), BF),
            pltpu.VMEM((DL, FL), BF),
            pltpu.VMEM((DL, FL), BF),
            pltpu.VMEM((FL, DL), BF),
            pltpu.VMEM((FL, DL), BF),
            pltpu.VMEM((DL, FL), F32),
            pltpu.VMEM((FL, DL), F32),
            pltpu.VMEM((TB, FL), F32),
            pltpu.VMEM((2, plan.long + 3, TB, FL), BF),
            pltpu.VMEM((NZ, TL, DL), BF),
            pltpu.VMEM((NZ, TL, DL), BF),
            pltpu.VMEM((NZ, TL, DL), BF),
            pltpu.VMEM((Y, X, TL // 2, DL), BF),
            pltpu.VMEM((X, Y, TL // 2, DL), BF),
            pltpu.VMEM((Y, TL // 2, DL), BF),
            pltpu.VMEM((X, TL // 2, DL), BF),
            pltpu.VMEM((Y, TL // 2, DL), BF),
            pltpu.VMEM((X, TL // 2, DL), BF),
            dma((15,)),
            dma((10,)),
            dma((msgs, plan.subs_act)),
            dma((2, plan.long + 2, plan.subs_rs)),
            dma((msgs, plan.subs_del)),
        ]
        + [dma((nq,))] * 7
        + [dma((Y, X)), dma((X, Y)), dma((Y,)), dma((X,))],
        compiler_params=pltpu.CompilerParams(
            collective_id=plan.call, has_side_effects=True, vmem_limit_bytes=60 * 1024 * 1024
        ),
    )(*operands)


def hand_over(*refs):
    n = (len(refs) - 2) // 3
    sources, targets, held, (came, left) = refs[:n], refs[n : 2 * n], refs[2 * n : 3 * n], refs[3 * n :]
    loads = [pltpu.make_async_copy(sources[k], held[k], came.at[k]) for k in range(n)]
    stores = [pltpu.make_async_copy(held[k], targets[k], left.at[k]) for k in range(n)]
    for load in loads:
        load.start()
    for load, store in zip(loads, stores):
        load.wait()
        store.start()
    for store in stores:
        store.wait()


def results(*arrays):
    hbm = pl.BlockSpec(memory_space=pltpu.HBM)
    n = len(arrays)
    return pl.pallas_call(
        hand_over,
        out_shape=tuple(jax.ShapeDtypeStruct(a.shape, a.dtype) for a in arrays),
        in_specs=[hbm] * n,
        out_specs=(hbm,) * n,
        scratch_shapes=[pltpu.VMEM(a.shape, a.dtype) for a in arrays] + [pltpu.SemaphoreType.DMA((n,))] * 2,
        compiler_params=pltpu.CompilerParams(vmem_limit_bytes=60 * 1024 * 1024),
    )(*arrays)


def shards(
    plan, inputs, out_grad, preact, weight_in, weight_out, moment_in, second_in, moment_out, second_out
):
    return results(
        *exchange(
            plan,
            out_grad,
            inputs,
            preact,
            weight_in,
            weight_out,
            moment_in,
            second_in,
            moment_out,
            second_out,
        )
    )


def solution(mesh):
    n_row, n_col = mesh.shape["row"], mesh.shape["col"]

    def whole(inputs, out_grad, preact, *rest):
        plan = Plan(
            n_row, n_col, inputs.shape[0] // n_row, inputs.shape[1] // n_col, preact.shape[1] // n_row
        )
        by_token, by_weight = P("row", "col"), P("col", "row")
        return jax.shard_map(
            functools.partial(shards, plan),
            mesh=mesh,
            in_specs=(
                by_token,
                by_token,
                by_weight,
                by_weight,
                by_token,
                by_weight,
                by_weight,
                by_token,
                by_token,
            ),
            out_specs=(by_token, by_weight, by_weight, by_weight, by_token, by_token, by_token),
            check_vma=False,
        )(inputs, out_grad, preact, *rest)

    return whole
```

```python
import functools
import math

import jax
import jax.numpy as jnp
from jax import lax
from jax.experimental import pallas as pl
from jax.experimental.pallas import tpu as pltpu
from jax.sharding import PartitionSpec as P

gelu_coef = 0.7978845608
beta_first = 0.9
beta_second = 0.95
learn_rate = 0.003
epsilon_adam = 1e-08
correct_first = 1.0 - 0.9**10
correct_second = 1.0 - 0.95**10

MESH = pl.DeviceIdType.MESH
BF = jnp.bfloat16
F32 = jnp.float32


def PEERS(n):
    return (1, n - 1) + tuple(range(2, n - 1)) if n > 2 else (1,)


def gelu_parts(preact):
    values = preact.astype(jnp.float32)
    tangent = jnp.tanh(gelu_coef * (values + 0.044715 * values * values * values))
    activated = 0.5 * values * (1.0 + tangent)
    slopes = 0.5 * (1.0 + tangent) + 0.5 * values * (1.0 - tangent * tangent) * gelu_coef * (
        1.0 + 3.0 * 0.044715 * values * values
    )
    return (activated, slopes)


def adam_step(weight, moment, second, grads):
    first_new = beta_first * moment.astype(jnp.float32) + (1.0 - beta_first) * grads
    second_new = beta_second * second.astype(jnp.float32) + (1.0 - beta_second) * grads * grads
    weight_new = weight.astype(jnp.float32) - learn_rate * (first_new / correct_first) / (
        jnp.sqrt(second_new / correct_second) + epsilon_adam
    )
    return (
        weight_new.astype(jnp.bfloat16),
        first_new.astype(jnp.bfloat16),
        second_new.astype(jnp.bfloat16),
    )


def nt_dot(left, right):
    return lax.dot_general(left, right, (((1,), (1,)), ((), ())), preferred_element_type=F32)


def tn_dot(left, right):
    return lax.dot_general(left, right, (((0,), (0,)), ((), ())), preferred_element_type=F32)


class Plan:
    def __init__(self, n_row, n_col, tokens, features, hidden):
        self.nq = n_row // 2
        self.X = math.isqrt(self.nq)
        self.Y = self.nq // self.X
        self.nz = n_col
        self.long = n_col // 2
        self.short = n_col - 1 - self.long
        self.msgs = n_col - 1
        self.TL = tokens
        self.TB = 2 * tokens
        self.DL = features
        self.FL = hidden
        self.subs_act, self.subs_rs = 2, 4
        self.subs_del = self.subs_rs
        self.act_1, self.act_2, self.act_3, self.act_every = 2, 2, 10, 2
        self.lag1, self.lag2 = 3, 6
        self.jump_rs, self.jump_del = 1, 1
        self.lead, self.in_1, self.early, self.act_4 = 1, 2, 5, 11
        self.adam_rows = 32
        self.ops = 2
        self.call = 0


def kernel(
    plan,
    og_ref,
    in_ref,
    pre_ref,
    win_ref,
    wout_ref,
    moment_in_ref,
    second_in_ref,
    moment_out_ref,
    second_out_ref,
    ig_ref,
    new_win_ref,
    new_moment_in_ref,
    new_second_in_ref,
    new_wout_ref,
    new_moment_out_ref,
    new_second_out_ref,
    og_all,
    in_all,
    act_all,
    del_all,
    pre,
    win,
    wout,
    moments_in,
    seconds_in,
    moments_out,
    seconds_out,
    gin_ref,
    gout_ref,
    slopes,
    ring,
    sib_out,
    sib_in,
    own,
    rv_a,
    rv_b,
    st_a,
    st_b,
    fin_a,
    fin_b,
    load,
    sent,
    act_r,
    rs_r,
    del_r,
    og_a_r,
    og_b_r,
    og_sib_r,
    in_a_r,
    in_b_r,
    in_sib_r,
    sib_r,
    ra_r,
    rb_r,
    fa_r,
    fb_r,
):
    X, Y, NZ, TL, TB = plan.X, plan.Y, plan.nz, plan.TL, plan.TB
    HALF, MSGS = TL // 2, plan.msgs
    r = lax.axis_index("row")
    z = lax.axis_index("col")

    def div(a, n):
        if isinstance(a, int):
            return a // n
        if plan.ops == 2 and n & (n - 1) == 0:
            return lax.shift_right_logical(a, jnp.int32(n.bit_length() - 1))
        return lax.div(a, jnp.int32(n)) if plan.ops else a // n

    def mod(a, n):
        if isinstance(a, int):
            return a % n
        if plan.ops == 2 and n & (n - 1) == 0:
            return a & (n - 1)
        return lax.rem(a, jnp.int32(n)) if plan.ops else a % n

    q = div(r, 2)
    c = mod(r, 2)
    x = div(q, Y)
    y = mod(q, Y)
    sgn = 1 - 2 * c
    sib = (r + sgn, z)
    OG, IN, ACT, RS, DEL, SIB, RA, RB, FA, FB = (sent.at[k] for k in range(10))

    def chip(cx, cy):
        return ((cx * Y + cy) * 2 + c, z)

    def x_peer(j):
        return mod(x + j, X)

    def y_peer(j):
        return mod(y + j, Y)

    def remote(src, dst, ssem, rsem, dev):
        return pltpu.make_async_remote_copy(
            src_ref=src, dst_ref=dst, send_sem=ssem, recv_sem=rsem, device_id=dev, device_id_type=MESH
        )

    def rows(buf, start, size):
        return buf.at[pl.ds(pl.multiple_of(start, 16), size)]

    def sign(n):
        return (1 - 2 * mod(n, 2)) * sgn

    def plane(step):
        return (r, mod(z + step + NZ, NZ))

    def at_step(i, a):
        return jnp.where(i == a, 1, 0)

    class Ring:
        def __init__(self, buf, jump, subs, ssem, rsem):
            self.buf, self.jump, self.subs, self.ssem, self.rsem = buf, jump, subs, ssem, rsem

        def copy(self, block, n, sub, hops):
            size = TB // self.subs
            part = rows(self.buf, block * TB + sub * size, size)
            return remote(part, part, self.ssem, self.rsem.at[n, sub], plane(sign(n) * hops))

        def start(self, sub):
            for dist in (1, self.jump) if self.jump > 1 else (1,):
                for n in (2 * dist - 2, 2 * dist - 1):
                    self.copy(z, n, sub, dist).start()

        def passed(self, n):
            block = mod(z - sign(n) * (div(n, 2) + 1) + 2 * NZ, NZ)
            for sub in range(self.subs):
                self.copy(block, n, sub, 1).wait_recv()

                @pl.when((n + 2 < MSGS) & (div(n, 2) + 2 != (self.jump if self.jump > 1 else 0)))
                def _():
                    self.copy(block, n + 2, sub, 1).start()

    acts = Ring(act_all, 1, plan.subs_act, ACT, act_r)
    deltas = Ring(del_all, plan.jump_del, plan.subs_del, DEL, del_r)

    def block_rows(buf, cx, cy, part=None, core=None):
        start = ((cx * Y + cy) * 2 + (c if core is None else core)) * TL
        if part is None:
            return rows(buf, start, TL)
        return rows(buf, start + part * HALF, HALF)

    class Gather:
        def __init__(self, source, buf, ssem, a_r, b_r, s_r):
            self.source, self.buf, self.ssem, self.a_r, self.b_r, self.s_r = source, buf, ssem, a_r, b_r, s_r

        def copy(self, cx, cy, part, sem, dev, core=None):
            ref = block_rows(self.buf, cx, cy, part, core)
            return remote(ref, ref, self.ssem, sem.at[cx * Y + cy], dev)

        def to_sib(self, cx, cy):
            return self.copy(cx, cy, None, self.s_r, sib)

        def from_sib(self, cx, cy):
            return self.copy(cx, cy, None, self.s_r, sib, 1 - c)

        def first(self):
            ref = block_rows(self.buf, x, y)
            for j in PEERS(X):
                remote(self.source, ref, self.ssem, self.a_r.at[q], chip(x_peer(j), y)).start()
            for j in PEERS(Y):
                remote(self.source, ref, self.ssem, self.a_r.at[q], chip(x, y_peer(j))).start()
            remote(self.source, ref, self.ssem, self.s_r.at[q], sib).start()

        def second_a(self, cx):
            self.copy(cx, y, None, self.a_r, sib).wait_recv()
            for k in PEERS(Y):
                self.copy(cx, y, 0, self.a_r, chip(x, y_peer(k))).start()
            self.to_sib(cx, y).start()

        def second_b(self, cy):
            self.copy(x, cy, None, self.a_r, sib).wait_recv()
            for k in PEERS(X):
                self.copy(x, cy, 1, self.b_r, chip(x_peer(k), y)).start()
            self.to_sib(x, cy).start()

        def third(self, cx, cy):
            self.copy(cx, cy, 0, self.a_r, sib).wait_recv()
            self.copy(cx, cy, 1, self.b_r, sib).wait_recv()
            self.to_sib(cx, cy).start()

        def sent(self):
            size = (X + Y - 2) * TL + (X - 1) * (Y - 1) * 2 * HALF + X * Y * TL
            whole = rows(self.buf, 0, size)
            remote(whole, whole, self.ssem, self.s_r.at[0], sib).wait_send()

    THIRDS = (X - 1) * (Y - 1)
    og = Gather(og_ref, og_all, OG, og_a_r, og_b_r, og_sib_r)
    inp = Gather(in_ref, in_all, IN, in_a_r, in_b_r, in_sib_r)

    def loop(low, high, body):
        def step(i, _):
            body(i)
            return 0

        lax.fori_loop(low, high, step, 0)

    barrier = pltpu.get_barrier_semaphore()
    friends = [sib]
    for hops in sorted({1, plan.jump_rs, plan.jump_del}):
        friends += [plane(hops), plane(-hops)]
    friends += [chip(x_peer(j), y) for j in range(1, X)]
    friends += [chip(x, y_peer(j)) for j in range(1, Y)]
    for friend in friends:
        pl.semaphore_signal(barrier, inc=1, device_id=friend, device_id_type=MESH)
    get_pre = pltpu.make_async_copy(pre_ref, pre, load.at[0])
    get_og = pltpu.make_async_copy(og_ref, rows(og_all, r * TL, TL), load.at[1])
    get_wout = pltpu.make_async_copy(wout_ref, wout, load.at[2])
    get_in = pltpu.make_async_copy(in_ref, rows(in_all, r * TL, TL), load.at[3])
    get_win = pltpu.make_async_copy(win_ref, win, load.at[4])
    get_adam = [
        pltpu.make_async_copy(ref, buf, load.at[5 + k])
        for k, (ref, buf) in enumerate(
            (
                (moment_out_ref, moments_out),
                (second_out_ref, seconds_out),
                (moment_in_ref, moments_in),
                (second_in_ref, seconds_in),
            )
        )
    ]
    for get in [get_og, get_pre, get_wout, get_in, get_win] + get_adam:
        get.start()
    block = pl.ds(pl.multiple_of(z * TB, 16), TB)
    LONG, SHORT, JUMP = plan.long, plan.short, plan.jump_rs
    FAR, OWN = LONG + 1, LONG + 2
    fresh = [(0, LONG), (1, SHORT), (1, OWN)]
    if JUMP > 1:
        fresh += [(0, JUMP - 1), (1, JUMP - 1)]
    for way, slot in fresh:
        ring[way, slot] = jnp.zeros((TB, plan.FL), BF)
    gin_ref[...] = jnp.zeros_like(gin_ref)
    gout_ref[...] = jnp.zeros_like(gout_ref)
    pl.semaphore_wait(barrier, len(friends))

    late = jnp.minimum(mod(q - z + NZ, NZ), mod(z - q + NZ, NZ)) < plan.early

    @pl.when(jnp.logical_not(late))
    def _():
        og.first()

    get_pre.wait()
    act, slope = gelu_parts(pre[...])
    act_all[block] = act.astype(BF)
    for sub in range(plan.subs_act):
        acts.start(sub)

    @pl.when(late)
    def _():
        og.first()

    slopes[...] = slope
    get_og.wait()
    get_in.wait()
    get_wout.wait()
    get_win.wait()

    def needed(n):
        way = mod(n, 2)
        k = div(n, 2) + way
        dist = LONG - k
        if JUMP > 1:
            dist = dist - at_step(k, LONG - JUMP) + at_step(k, LONG - JUMP + 1)
        return way, dist, mod(z + (1 - 2 * way) * sgn * dist + NZ, NZ)

    def og_near(n):
        t = needed(n)[2]
        tx, ty = div(t, Y), mod(t, Y)

        @pl.when((tx != x) & (ty == y))
        def _():
            og.second_a(tx)

        @pl.when((tx == x) & (ty != y))
        def _():
            og.second_b(ty)

    def og_far(n):
        t = needed(n)[2]
        tx, ty = div(t, Y), mod(t, Y)

        @pl.when((tx != x) & (ty != y))
        def _():
            og.third(tx, ty)

    LEAD = plan.lead
    loop(0, NZ, og_near)
    loop(0, plan.act_1, acts.passed)
    loop(0, LEAD, og_far)
    loop(plan.act_1, plan.act_2, acts.passed)

    def rs_copy(way, dist, sub):
        size = TB // plan.subs_rs
        here = pl.ds(sub * size, size)
        direct = at_step(dist, JUMP)
        into = dist - 1 + direct * (FAR - JUMP + 1)
        hops = 1 + direct * (JUMP - 1)
        return remote(
            ring.at[way, dist, here],
            ring.at[way, into, here],
            RS,
            rs_r.at[way, into, sub],
            plane((1 - 2 * way) * sgn * hops),
        )

    def rs_got(way, slot, sub):
        size = TB // plan.subs_rs
        ref = ring.at[way, slot, pl.ds(sub * size, size)]
        return remote(ref, ref, RS, rs_r.at[way, slot, sub], sib)

    def rs_step(n):
        way, dist, t = needed(n)

        @pl.when(n + LEAD < NZ)
        def _():
            og_far(n + LEAD)

        og.from_sib(div(t, Y), mod(t, Y)).wait_recv()
        at = pl.multiple_of(t * TB, 16)
        part = nt_dot(og_all[pl.ds(at, TB)], wout[...]).astype(BF).astype(F32)
        size = TB // plan.subs_rs
        slot = jnp.where(dist == 0, OWN, dist)
        for sub in range(plan.subs_rs):
            here = pl.ds(sub * size, size)

            @pl.when((n >= 2) & (dist != (JUMP - 1 if JUMP > 1 else 0)) & (dist != 0))
            def _():
                rs_got(way, dist, sub).wait_recv()

            ring[way, slot, here] = (
                ring[way, slot, here].astype(F32) + part[sub * size : (sub + 1) * size]
            ).astype(BF)

            @pl.when(dist != 0)
            def _():
                rs_copy(way, dist, sub).start()

        m = plan.act_2 + div(n, plan.act_every)

        @pl.when((mod(n, plan.act_every) == plan.act_every - 1) & (m < plan.act_3))
        def _():
            acts.passed(m)

        @pl.when(n == plan.in_1)
        def _():
            inp.first()

        @pl.when((n > NZ - THIRDS - X) & (n < NZ - THIRDS))
        def _():
            j = n - (NZ - THIRDS - X)
            inp.second_a(x_peer(j))
            inp.second_b(y_peer(j))

        @pl.when((n >= NZ - THIRDS))
        def _():
            i = n - (NZ - THIRDS)
            inp.third(x_peer(div(i, Y - 1) + 1), y_peer(mod(i, Y - 1) + 1))

    loop(0, NZ, rs_step)
    size = TB // plan.subs_rs
    for sub in range(plan.subs_rs):
        here = pl.ds(sub * size, size)
        total = ring[1, OWN, here].astype(F32)
        for slot in (0, FAR) if JUMP > 1 else (FAR,):
            for way in (0, 1):
                rs_got(way, slot, sub).wait_recv()
                total = total + ring[way, slot, here].astype(F32)
        piece = pl.ds(pl.multiple_of(z * TB + sub * size, 16), size)
        del_all[piece] = (total * slopes[here]).astype(BF)
        deltas.start(sub)
    loop(0, X * Y, lambda i: inp.from_sib(div(i, Y), mod(i, Y)).wait_recv())

    def far(i):
        k = div(i + 1, 2)
        return k + at_step(k, 2) - at_step(k, 3) if plan.jump_del == 3 else k

    def message(i):
        return 2 * far(i) - 1 - mod(i, 2)

    def token_block(i, hops):
        sig = (2 * mod(i, 2) - 1) * sgn
        return mod(z - sig * hops + 2 * NZ, NZ)

    def chunk(i):
        return token_block(i, far(i))

    def sib_copy(t):
        return remote(sib_out.at[t], sib_in.at[t], SIB, sib_r.at[t], sib)

    low, high = pl.ds(0, HALF), pl.ds(HALF, HALF)

    def a_copy(t):
        tx, ty = div(t, Y), mod(t, Y)
        return remote(own.at[t, low], rv_a.at[ty, x], RA, ra_r.at[ty, x], chip(tx, y))

    def a_got(ty, sx):
        return remote(rv_a.at[ty, sx], rv_a.at[ty, sx], RA, ra_r.at[ty, sx], sib)

    def b_copy(t):
        tx, ty = div(t, Y), mod(t, Y)
        return remote(own.at[t, high], rv_b.at[tx, y], RB, rb_r.at[tx, y], chip(x, ty))

    def b_got(tx, sy):
        return remote(rv_b.at[tx, sy], rv_b.at[tx, sy], RB, rb_r.at[tx, sy], sib)

    def fa_copy(ty):
        return remote(st_a.at[ty], fin_a.at[y], FA, fa_r.at[y], chip(x, ty))

    def fb_copy(tx):
        return remote(st_b.at[tx], fin_b.at[x], FB, fb_r.at[x], chip(tx, y))

    def arrive(i):
        @pl.when(i >= 1)
        def _():
            deltas.passed(message(i))

        t = chunk(i)
        at = pl.multiple_of(t * TB, 16)
        here = pl.ds(at, TB)
        both = nt_dot(del_all[here], win[...]).astype(BF)
        halves = (both[:TL], both[TL:])
        sib_out[t] = jnp.where(c == 0, halves[1], halves[0])
        sib_copy(t).start()
        own[t] = jnp.where(c == 0, halves[0], halves[1])
        gin_ref[...] += tn_dot(in_all[here], del_all[here])

    def add_out(i):
        here = pl.ds(pl.multiple_of(token_block(i, div(i + 1, 2)) * TB, 16), TB)
        gout_ref[...] += tn_dot(act_all[here], og_all[here])

    def pair(i):
        t = chunk(i)
        sib_copy(t).wait_recv()
        own[t] = (own[t].astype(F32) + sib_in[t].astype(F32)).astype(BF)

        @pl.when(div(t, Y) != x)
        def _():
            a_copy(t).start()

        @pl.when(mod(t, Y) != y)
        def _():
            b_copy(t).start()

    def line(i):
        t = chunk(i)
        tx, ty = div(t, Y), mod(t, Y)

        @pl.when(tx == x)
        def _():
            total = own[t, low].astype(F32)
            for j in range(1, X):
                a_got(ty, x_peer(j)).wait_recv()
                total = total + rv_a[ty, x_peer(j)].astype(F32)
            st_a[ty] = total.astype(BF)

            @pl.when(ty != y)
            def _():
                fa_copy(ty).start()

        @pl.when(ty == y)
        def _():
            total = own[t, high].astype(F32)
            for j in range(1, Y):
                b_got(tx, y_peer(j)).wait_recv()
                total = total + rv_b[tx, y_peer(j)].astype(F32)
            st_b[tx] = total.astype(BF)

            @pl.when(tx != x)
            def _():
                fb_copy(tx).start()

    ROWS = plan.adam_rows

    def adam(weight, moment, second, grads, low, high):
        def some(k):
            here = pl.ds(pl.multiple_of(k * ROWS, ROWS), ROWS)
            new = adam_step(weight[here], moment[here], second[here], grads[here])
            weight[here], moment[here], second[here] = new

        loop(low, high, some)

    put_out = [
        pltpu.make_async_copy(buf, ref, load.at[9 + k])
        for k, (ref, buf) in enumerate(
            ((new_wout_ref, wout), (new_moment_out_ref, moments_out), (new_second_out_ref, seconds_out))
        )
    ]
    put_in = [
        pltpu.make_async_copy(buf, ref, load.at[12 + k])
        for k, (ref, buf) in enumerate(
            ((new_win_ref, win), (new_moment_in_ref, moments_in), (new_second_in_ref, seconds_in))
        )
    ]

    LAG1, LAG2 = plan.lag1, plan.lag2

    def del_step(i):
        arrive(i)

        @pl.when(i <= plan.act_3)
        def _():
            add_out(i)

        @pl.when((i >= plan.act_4) & (i < plan.act_4 + MSGS - plan.act_3))
        def _():
            acts.passed(plan.act_3 + i - plan.act_4)
            add_out(plan.act_3 + i - plan.act_4 + 1)

        @pl.when(i >= LAG1)
        def _():
            pair(i - LAG1)

        @pl.when(i >= LAG2)
        def _():
            line(i - LAG2)

    loop(0, NZ, del_step)
    for get in get_adam:
        get.wait()
    loop(NZ - LAG1, NZ, pair)
    loop(NZ - LAG2, NZ - 1, line)
    adam(wout, moments_out, seconds_out, gout_ref, 0, plan.FL // ROWS)
    for put in put_out:
        put.start()
    blocks = plan.DL // ROWS
    adam(win, moments_in, seconds_in, gin_ref, 0, blocks // 4)
    line(NZ - 1)
    adam(win, moments_in, seconds_in, gin_ref, blocks // 4, blocks)
    for put in put_in:
        put.start()

    og.sent()
    inp.sent()
    messages = rows(act_all, 0, MSGS * TB)
    remote(messages, messages, ACT, act_r.at[0, 0], sib).wait_send()
    remote(messages, messages, DEL, del_r.at[0, 0], sib).wait_send()
    remote(messages, messages, RS, act_r.at[0, 0], sib).wait_send()
    remote(sib_out, sib_out, SIB, sib_r.at[0], sib).wait_send()
    halves = sib_out.at[pl.ds(0, (X - 1) * Y // 2)]
    remote(halves, halves, RA, sib_r.at[0], sib).wait_send()
    halves = sib_out.at[pl.ds(0, (Y - 1) * X // 2)]
    remote(halves, halves, RB, sib_r.at[0], sib).wait_send()

    total = st_a[y].astype(F32)
    for j in range(1, Y):
        remote(fin_a.at[y_peer(j)], fin_a.at[y_peer(j)], FA, fa_r.at[y_peer(j)], sib).wait_recv()
        total = total + fin_a[y_peer(j)].astype(F32)
    ig_ref[low] = total.astype(BF)
    total = st_b[x].astype(F32)
    for j in range(1, X):
        remote(fin_b.at[x_peer(j)], fin_b.at[x_peer(j)], FB, fb_r.at[x_peer(j)], sib).wait_recv()
        total = total + fin_b[x_peer(j)].astype(F32)
    ig_ref[high] = total.astype(BF)
    for put in put_out + put_in:
        put.wait()
    last = st_a.at[pl.ds(0, Y - 1)]
    remote(last, last, FA, fa_r.at[0], sib).wait_send()
    last = st_b.at[pl.ds(0, X - 1)]
    remote(last, last, FB, fb_r.at[0], sib).wait_send()


def exchange(plan, *operands):
    X, Y, NZ, TL, TB, DL, FL = plan.X, plan.Y, plan.nz, plan.TL, plan.TB, plan.DL, plan.FL
    nq, msgs = plan.nq, plan.msgs
    dma = pltpu.SemaphoreType.DMA
    vmem = pl.BlockSpec(memory_space=pltpu.VMEM)
    hbm = pl.BlockSpec(memory_space=pltpu.HBM)
    return pl.pallas_call(
        functools.partial(kernel, plan),
        out_shape=(jax.ShapeDtypeStruct((TL, DL), BF),)
        + (jax.ShapeDtypeStruct((DL, FL), BF),) * 3
        + (jax.ShapeDtypeStruct((FL, DL), BF),) * 3,
        in_specs=[hbm] * 9,
        out_specs=(vmem,) + (hbm,) * 6,
        scratch_shapes=[
            pltpu.VMEM((nq * TB, DL), BF),
            pltpu.VMEM((nq * TB, DL), BF),
            pltpu.VMEM((NZ * TB, FL), BF),
            pltpu.VMEM((NZ * TB, FL), BF),
            pltpu.VMEM((TB, FL), BF),
            pltpu.VMEM((DL, FL), BF),
            pltpu.VMEM((FL, DL), BF),
            pltpu.VMEM((DL, FL), BF),
            pltpu.VMEM((DL, FL), BF),
            pltpu.VMEM((FL, DL), BF),
            pltpu.VMEM((FL, DL), BF),
            pltpu.VMEM((DL, FL), F32),
            pltpu.VMEM((FL, DL), F32),
            pltpu.VMEM((TB, FL), F32),
            pltpu.VMEM((2, plan.long + 3, TB, FL), BF),
            pltpu.VMEM((NZ, TL, DL), BF),
            pltpu.VMEM((NZ, TL, DL), BF),
            pltpu.VMEM((NZ, TL, DL), BF),
            pltpu.VMEM((Y, X, TL // 2, DL), BF),
            pltpu.VMEM((X, Y, TL // 2, DL), BF),
            pltpu.VMEM((Y, TL // 2, DL), BF),
            pltpu.VMEM((X, TL // 2, DL), BF),
            pltpu.VMEM((Y, TL // 2, DL), BF),
            pltpu.VMEM((X, TL // 2, DL), BF),
            dma((15,)),
            dma((10,)),
            dma((msgs, plan.subs_act)),
            dma((2, plan.long + 2, plan.subs_rs)),
            dma((msgs, plan.subs_del)),
        ]
        + [dma((nq,))] * 7
        + [dma((Y, X)), dma((X, Y)), dma((Y,)), dma((X,))],
        compiler_params=pltpu.CompilerParams(
            collective_id=plan.call, has_side_effects=True, vmem_limit_bytes=60 * 1024 * 1024
        ),
    )(*operands)


def hand_over(*refs):
    n = (len(refs) - 2) // 3
    sources, targets, held, (came, left) = refs[:n], refs[n : 2 * n], refs[2 * n : 3 * n], refs[3 * n :]
    loads = [pltpu.make_async_copy(sources[k], held[k], came.at[k]) for k in range(n)]
    stores = [pltpu.make_async_copy(held[k], targets[k], left.at[k]) for k in range(n)]
    for load in loads:
        load.start()
    for load, store in zip(loads, stores):
        load.wait()
        store.start()
    for store in stores:
        store.wait()


def results(*arrays):
    hbm = pl.BlockSpec(memory_space=pltpu.HBM)
    n = len(arrays)
    return pl.pallas_call(
        hand_over,
        out_shape=tuple(jax.ShapeDtypeStruct(a.shape, a.dtype) for a in arrays),
        in_specs=[hbm] * n,
        out_specs=(hbm,) * n,
        scratch_shapes=[pltpu.VMEM(a.shape, a.dtype) for a in arrays] + [pltpu.SemaphoreType.DMA((n,))] * 2,
        compiler_params=pltpu.CompilerParams(vmem_limit_bytes=60 * 1024 * 1024),
    )(*arrays)


def shards(
    plan, inputs, out_grad, preact, weight_in, weight_out, moment_in, second_in, moment_out, second_out
):
    return results(
        *exchange(
            plan,
            out_grad,
            inputs,
            preact,
            weight_in,
            weight_out,
            moment_in,
            second_in,
            moment_out,
            second_out,
        )
    )


def solution(mesh):
    n_row, n_col = mesh.shape["row"], mesh.shape["col"]

    def whole(inputs, out_grad, preact, *rest):
        plan = Plan(
            n_row, n_col, inputs.shape[0] // n_row, inputs.shape[1] // n_col, preact.shape[1] // n_row
        )
        by_token, by_weight = P("row", "col"), P("col", "row")
        return jax.shard_map(
            functools.partial(shards, plan),
            mesh=mesh,
            in_specs=(
                by_token,
                by_token,
                by_weight,
                by_weight,
                by_token,
                by_weight,
                by_weight,
                by_token,
                by_token,
            ),
            out_specs=(by_token, by_weight, by_weight, by_weight, by_token, by_token, by_token),
            check_vma=False,
        )(inputs, out_grad, preact, *rest)

    return whole
```
